32 devices in a mesh: group: 2 (over y), pitch: 4 (over z), span: 2 (over x), radial: 2 (over core).
Axes of the slice: x: 2, y: 2, z: 4, core: 2. Of those that a mesh axis runs over, the one named last changes fastest.
Arguments:
- state: float32 [14, 6, 16, 8, 256], P('group', None, 'pitch', 'span', 'radial'), parts along dimension 0, may hold values from -0.5 to 2.8, as said below
- adjoint: float32 [14, 6, 16, 8, 256], P('group', None, 'pitch', 'span', 'radial'), parts along dimension 0, may hold values from -6 to 6
- displacement: float32 [6, 16, 8, 256], P('group', 'pitch', 'span', 'radial'), parts along dimension 0, may hold values from -0.1 to 0.1
Outputs:
- adjoint_residual: float32 [14, 6, 16, 8, 256], P('group', None, 'pitch', 'span', 'radial'), parts along dimension 0
- mesh_sensitivity: float32 [6, 16, 8, 256], P('group', 'pitch', 'span', 'radial'), parts along dimension 0
The draws below stay inside these ranges and needn't reach their ends.
There are 2 independent parts, one for each index of `group`. The reference program is written for one: setup_inputs(seed, part) draws one part's arguments, and reference() takes and returns one part's arrays. A program takes and returns all parts, laid end to end along the dimension named above; each array names one. Nothing has to cross between parts.
Inputs may be any that keep to these rules, and one draw needn't show every extreme that they name: `state`: density within 0.8 to 1.2, momenta within -0.5 to 0.5, energy within 2.2 to 2.8, turbulence variable within 0.05 to 0.15.
All inputs are finite; a program needn't handle non-finite values.
Results may differ from the reference program's by a relative error of at most 0.0003.
Values sent between devices are 32-bit elements; how exact they have to be, the bound alone decides.
A program may use at most 64 MiB of HBM per device.

```python
import jax
import jax.numpy as jnp
from jax import lax

NT = 7
NV = 6
NP = 16
NS = 8
NR = 256


def draw_state(key, part):
    key = jax.random.fold_in(key, 11)
    unit = jax.random.uniform(key, (NT, NV, NP, NS, NR), jnp.float32)
    lower = jnp.array([0.8, -0.5, -0.5, -0.5, 2.2, 0.05], jnp.float32)
    extent = jnp.array([0.4, 1.0, 1.0, 1.0, 0.6, 0.1], jnp.float32)
    return lower[None, :, None, None, None] + extent[None, :, None, None, None] * unit


def steps_of(stream_key, shape, cuts, smallest, high):
    factor_of = 1.0
    for position, shards_of in cuts:
        heights = jax.random.uniform(jax.random.fold_in(jax.random.fold_in(stream_key, 6), position), (shards_of,), jnp.float32, smallest / len(cuts), high / len(cuts))
        factor_of = factor_of * jnp.repeat(jnp.exp(heights), shape[position] // shards_of).reshape((-1,) + (1,) * (len(shape) - 1 - position))
    return factor_of


def centred(own_key, shape, scale, reach, split=(), held_as=jnp.bfloat16):
    level = steps_of(own_key, shape, split, -0.22, 0.18) if split else 1.0
    values = jax.random.normal(own_key, shape, jnp.float32) * scale * level
    return jnp.minimum(jnp.maximum(values, -reach), reach).astype(held_as)


def setup_inputs(seed: int = 0, part: int = 0) -> dict:
    arg_keys = jax.random.split(jax.random.key(seed), 4)
    own_keys = jax.random.split(jax.random.fold_in(arg_keys[3], part), 4)
    state = draw_state(jax.random.fold_in(jax.random.fold_in(arg_keys[3], part), 71), part)
    adjoint = centred(own_keys[1], (NT, NV, NP, NS, NR), 1.0, 6.0, ((2, 4), (3, 2), (4, 2)), jnp.float32)
    displacement = jnp.clip(jax.random.uniform(own_keys[2], (3, NP, NS, NR), jnp.float32, -0.1, 0.1) * steps_of(own_keys[2], (3, NP, NS, NR), ((1, 4), (2, 2), (3, 2)), -0.4, 0.0), -0.1, 0.1)
    return {"state": state, "adjoint": adjoint, "displacement": displacement}


LAMINAR_MU = 0.02
CV_CUBE = 7.1 ** 3
SECOND_COEFF = 0.5
FOURTH_COEFF = 1.0 / 32.0
HEAT_DIFFUSIVE = 4.86
SIGMA_TURB = 2.0 / 3.0
PRODUCTION_COEF = 0.1355
CW_ONE = 3.24
FREQUENCY = 1.0

def spectral():
    steps = jnp.arange(NT, dtype=jnp.float32)
    gap = steps[:, None] - steps[None, :]
    safe = jnp.where(gap == 0, 1.0, gap)
    return jnp.where(gap == 0, 0.0, 0.5 * jnp.cos(jnp.pi * safe) / jnp.sin(jnp.pi * safe / NT))

def clipping_tolerance(array, keep):
    for streamwise_coordinate in range(3):
        if streamwise_coordinate != keep:
            dim = array.ndim - 3 + streamwise_coordinate
            array = lax.slice_in_dim(array, 2, array.shape[dim] - 2, axis=dim)
    return array

def window(array, streamwise_coordinate, start, stop_back):
    dim = array.ndim - 3 + streamwise_coordinate
    return lax.slice_in_dim(array, start, array.shape[dim] - stop_back, axis=dim)

def residual(flow_fields, wall):
    state_rows = NT * NV
    shape = flow_fields.shape[1:]
    conserved = flow_fields[:state_rows].reshape((NT, NV) + shape)
    moved = flow_fields[state_rows:]
    mass_per_volume = conserved[:, 0]
    momentum_vector = conserved[:, 1:4]
    energy = conserved[:, 4]
    working = conserved[:, 5]
    velocity = momentum_vector / mass_per_volume[:, None]
    thermodynamic_stress = 0.4 * (energy - 0.5 * lax.optimization_barrier(jnp.sum(momentum_vector * velocity, axis=1)))
    sound_speed = jnp.sqrt(1.4 * thermodynamic_stress / mass_per_volume)
    thermodynamic_heat_level = thermodynamic_stress / mass_per_volume
    ratio_cube = (mass_per_volume * working / LAMINAR_MU) ** 3
    viscosity = LAMINAR_MU + mass_per_volume * working * ratio_cube / (ratio_cube + CV_CUBE)
    total = None
    for streamwise_coordinate in range(3):
        cons = clipping_tolerance(conserved, streamwise_coordinate)
        vel = clipping_tolerance(velocity, streamwise_coordinate)
        pres = clipping_tolerance(thermodynamic_stress, streamwise_coordinate)
        sound = clipping_tolerance(sound_speed, streamwise_coordinate)
        damping_multiplier = clipping_tolerance(thermodynamic_heat_level, streamwise_coordinate)
        visc = clipping_tolerance(viscosity, streamwise_coordinate)
        dens = clipping_tolerance(mass_per_volume, streamwise_coordinate)
        turb = clipping_tolerance(working, streamwise_coordinate)
        shift = clipping_tolerance(moved[streamwise_coordinate], streamwise_coordinate)
        normal_vel = vel[:, streamwise_coordinate]
        press_unit = jnp.zeros((NV,), jnp.float32).at[1 + streamwise_coordinate].set(1.0)
        energy_unit = jnp.zeros((NV,), jnp.float32).at[4].set(1.0)
        cell_flux = normal_vel[:, None] * cons + pres[:, None] * press_unit[None, :, None, None, None] + (pres * normal_vel)[:, None] * energy_unit[None, :, None, None, None]
        left = lambda a: window(a, streamwise_coordinate, 1, 2)
        right = lambda a: window(a, streamwise_coordinate, 2, 1)
        central = 0.5 * (left(cell_flux) + right(cell_flux))
        second = window(pres, streamwise_coordinate, 2, 0) - 2.0 * window(pres, streamwise_coordinate, 1, 1) + window(pres, streamwise_coordinate, 0, 2)
        summed = window(pres, streamwise_coordinate, 2, 0) + 2.0 * window(pres, streamwise_coordinate, 1, 1) + window(pres, streamwise_coordinate, 0, 2)
        sensor = (second / summed) ** 2
        eps_two = SECOND_COEFF * 0.5 * (window(sensor, streamwise_coordinate, 0, 1) + window(sensor, streamwise_coordinate, 1, 0))
        eps_four = FOURTH_COEFF * FOURTH_COEFF / (FOURTH_COEFF + eps_two)
        radius = jnp.sqrt(normal_vel * normal_vel + 0.01) + sound
        spread = 0.5 * (left(radius) + right(radius))
        jump = right(cons) - left(cons)
        third = window(cons, streamwise_coordinate, 3, 0) - 3.0 * right(cons) + 3.0 * left(cons) - window(cons, streamwise_coordinate, 0, 3)
        dissip = (spread * eps_two)[:, None] * jump - (spread * eps_four)[:, None] * third
        spacing = 1.0 + right(shift) - left(shift)
        mu_face = 0.5 * (left(visc) + right(visc)) / spacing
        dvel = right(vel) - left(vel)
        energy_visc = mu_face * (0.5 * (lax.optimization_barrier(jnp.sum(right(vel) ** 2, axis=1)) - lax.optimization_barrier(jnp.sum(left(vel) ** 2, axis=1))) + HEAT_DIFFUSIVE * (right(damping_multiplier) - left(damping_multiplier)))
        turb_visc = (LAMINAR_MU + 0.5 * (left(dens * turb) + right(dens * turb))) / SIGMA_TURB / spacing * (right(turb) - left(turb))
        viscous = jnp.concatenate([jnp.zeros_like(mu_face)[:, None], mu_face[:, None] * dvel, energy_visc[:, None], turb_visc[:, None]], axis=1)
        face = central - dissip - viscous
        term = window(face, streamwise_coordinate, 1, 0) - window(face, streamwise_coordinate, 0, 1)
        total = term if total is None else total + term

    def gradient(comp, streamwise_coordinate):
        cut = clipping_tolerance(velocity[:, comp], streamwise_coordinate)
        return 0.5 * (window(cut, streamwise_coordinate, 3, 1) - window(cut, streamwise_coordinate, 1, 3))
    curl_x = gradient(2, 1) - gradient(1, 2)
    curl_y = gradient(0, 2) - gradient(2, 0)
    curl_z = gradient(1, 0) - gradient(0, 1)
    vorticity = jnp.sqrt(curl_x ** 2 + curl_y ** 2 + curl_z ** 2 + 0.01)
    volume = None
    for streamwise_coordinate in range(3):
        cut = clipping_tolerance(moved[streamwise_coordinate], streamwise_coordinate)
        factor = 1.0 + 0.5 * (window(cut, streamwise_coordinate, 3, 1) - window(cut, streamwise_coordinate, 1, 3))
        volume = factor if volume is None else volume * factor
    inner_cons = clipping_tolerance(conserved, -1)
    inner_dens = clipping_tolerance(mass_per_volume, -1)
    inner_turb = clipping_tolerance(working, -1)
    coupling = jnp.einsum('nm,mvabc->nvabc', spectral(), inner_cons, precision=lax.Precision.HIGHEST) * (FREQUENCY * volume)[None, None]
    source = -PRODUCTION_COEF * vorticity * inner_dens * inner_turb + CW_ONE * inner_dens * (inner_turb / wall) ** 2
    total = total + coupling
    total = total.at[:, 5].add(source)
    return total.reshape((state_rows,) + total.shape[2:])

def reference(state, adjoint, displacement):
    state_rows = NT * NV
    grid = state.shape[2:]
    positions = jnp.arange(grid[2], dtype=jnp.float32) + 0.5
    wall = jnp.minimum(positions, grid[2] - positions)

    def forward(stacked):
        padded = jnp.pad(stacked, ((0, 0), (2, 2), (0, 0), (0, 0)), mode='wrap')
        padded = jnp.pad(padded, ((0, 0), (0, 0), (2, 2), (0, 0)), mode='symmetric')
        padded = jnp.pad(padded, ((0, 0), (0, 0), (0, 0), (2, 2)), mode='symmetric')
        return residual(padded, wall)
    stacked = jnp.concatenate([state.reshape((state_rows,) + grid), displacement], axis=0)
    _, backward = jax.vjp(forward, stacked)
    result = backward(adjoint.reshape((state_rows,) + grid))[0]
    return (result[:state_rows].reshape(state.shape), result[state_rows:])
```

```python
import math

import jax
import jax.numpy as jnp
from jax import lax
from jax.experimental import pallas as pl
from jax.experimental.pallas import tpu as pltpu
from jax.sharding import PartitionSpec as P

NT = 7
NV = 6
LAMINAR_MU = 0.02
CV_CUBE = 7.1**3
SECOND_COEFF = 0.5
FOURTH_COEFF = 1.0 / 32.0
HEAT_DIFFUSIVE = 4.86
SIGMA_TURB = 2.0 / 3.0
PRODUCTION_COEF = 0.1355
CW_ONE = 3.24
FREQUENCY = 1.0
MESH = pl.DeviceIdType.MESH

CELLS = 16
ROWS = NV * CELLS
GROWS = NV * 8
PAD_STATE = (1.0, 0.0, 0.0, 0.0, 2.5, 0.1)


def coupling_matrix():
    out = [[0.0] * NT for _ in range(NT)]
    for n in range(NT):
        for m in range(NT):
            if n != m:
                out[n][m] = 0.5 * (-1.0) ** (n - m) / math.sin(math.pi * (n - m) / NT)
    return out


@jax.custom_jvp
def recip(x):
    return 1.0 / x


@recip.defjvp
def recip_jvp(primals, tangents):
    r = recip(primals[0])
    return r, -(r * r) * tangents[0]


@jax.custom_jvp
def root(x):
    return x * lax.rsqrt(x)


@root.defjvp
def root_jvp(primals, tangents):
    x = primals[0]
    y = lax.rsqrt(x)
    return x * y, (0.5 * y) * tangents[0]


def prim(u):
    inv = recip(u[0])
    vel = [u[1] * inv, u[2] * inv, u[3] * inv]
    kin = u[1] * vel[0] + u[2] * vel[1] + u[3] * vel[2]
    return inv, vel, 0.4 * (u[4] - 0.5 * kin)


def faces(d, cells, shift):
    n = len(cells)
    base = [prim(u) for u in cells]
    p = [b[2] for b in base]
    q = {}
    for i in range(1, n - 1):
        u = cells[i]
        inv, vel, pres = base[i]
        temp = pres * inv
        rn = u[0] * u[5]
        ratio = rn * (1.0 / LAMINAR_MU)
        cube = ratio * ratio * ratio
        visc = LAMINAR_MU + rn * (cube * recip(cube + CV_CUBE))
        un = vel[d]
        flux = [un * u[v] for v in range(NV)]
        flux[1 + d] = flux[1 + d] + pres
        flux[4] = flux[4] + pres * un
        radius = root(un * un + 0.01) + root(1.4 * temp)
        square = vel[0] * vel[0] + vel[1] * vel[1] + vel[2] * vel[2]
        ends = p[i + 1] + p[i - 1]
        ratio_p = (ends - 2.0 * pres) * recip(ends + 2.0 * pres)
        q[i] = (vel, temp, rn, visc, flux, radius, 0.5 * square + HEAT_DIFFUSIVE * temp, ratio_p * ratio_p)
    out = []
    for a in range(1, n - 2):
        b = a + 1
        qa, qb = q[a], q[b]
        eps_two = SECOND_COEFF * 0.5 * (qa[7] + qb[7])
        eps_four = FOURTH_COEFF * FOURTH_COEFF * recip(FOURTH_COEFF + eps_two)
        spread = 0.5 * (qa[5] + qb[5])
        two, four = spread * eps_two, spread * eps_four
        isp = recip(1.0 + shift[b] - shift[a])
        mu = 0.5 * (qa[3] + qb[3]) * isp
        turb = (LAMINAR_MU + 0.5 * (qa[2] + qb[2])) * (1.0 / SIGMA_TURB) * isp
        face = []
        for v in range(NV):
            jump = cells[b][v] - cells[a][v]
            third = cells[b + 1][v] - cells[a - 1][v] - 3.0 * jump
            f = 0.5 * (qa[4][v] + qb[4][v]) - two * jump + four * third
            if 1 <= v <= 3:
                f = f - mu * (qb[0][v - 1] - qa[0][v - 1])
            elif v == 4:
                f = f - mu * (qb[6] - qa[6])
            elif v == 5:
                f = f - turb * jump
            face.append(f)
        out.append(face)
    return out, q[1][4]


def source(pitch_up, pitch_dn, span_up, span_dn, rad_up, rad_dn, rho, nu, inv_wall):
    def gap(up, dn, k):
        return 0.5 * (up[k] * recip(up[0]) - dn[k] * recip(dn[0]))

    cx = gap(span_up, span_dn, 2) - gap(rad_up, rad_dn, 2)
    cy = gap(rad_up, rad_dn, 1) - gap(pitch_up, pitch_dn, 2)
    cz = gap(pitch_up, pitch_dn, 1) - gap(span_up, span_dn, 1)
    vort = root(cx * cx + cy * cy + cz * cz + 0.01)
    scaled = nu * inv_wall
    return rho * (CW_ONE * scaled * scaled - PRODUCTION_COEF * vort * nu)


def kernel(sizes, state, adjoint, disp, out_state, out_disp,
           own, lam, dis, other, other_lam, other_dis,
           pit_lo, pit_hi, spa_lo, spa_hi, dpit_lo, dpit_hi, dspa_lo, dspa_hi,
           send_lo, send_hi,
           upad, acc, gho, gacc, wbuf, dP, dS, dR, dG, cP, cS, cR, cG,
           rp_send_lo, rp_send_hi, rp_lo, rp_hi, rs_send_lo, rs_send_hi, rs_lo, rs_hi,
           rr_recv, rr_dsend, rr_drecv,
           local_sem, send_sem, recv_sem):
    n_pitch, n_span, n_rad, lanes = sizes
    ip = lax.axis_index("pitch")
    isp = lax.axis_index("span")
    ir = lax.axis_index("radial")
    ig = lax.axis_index("group")
    left = (ig, lax.rem(ip + n_pitch - 1, n_pitch), isp, ir)
    right = (ig, lax.rem(ip + 1, n_pitch), isp, ir)
    lower = (ig, ip, lax.rem(isp + n_span - 1, n_span), ir)
    upper = (ig, ip, lax.rem(isp + 1, n_span), ir)
    mate = (ig, ip, isp, 1 - ir)
    first = isp == 0
    last = isp == n_span - 1
    core0 = ir == 0

    loads = [
        pltpu.make_async_copy(adjoint, lam.at[pl.ds(0, NT * ROWS)], local_sem.at[1]),
        pltpu.make_async_copy(state, own.at[pl.ds(0, NT * ROWS)], local_sem.at[0]),
        pltpu.make_async_copy(disp, dis, local_sem.at[2]),
    ]
    for c in loads:
        c.start()

    bar = pltpu.get_barrier_semaphore()
    for who in (left, right, mate):
        pl.semaphore_signal(bar, inc=1, device_id=who, device_id_type=MESH)

    @pl.when(jnp.logical_not(first))
    def _():
        pl.semaphore_signal(bar, inc=1, device_id=lower, device_id_type=MESH)

    @pl.when(jnp.logical_not(last))
    def _():
        pl.semaphore_signal(bar, inc=1, device_id=upper, device_id_type=MESH)

    loads[1].wait()
    zero8 = jnp.zeros((8, lanes), jnp.float32)
    for v in range(NV):
        const = jnp.full((8, lanes), PAD_STATE[v], jnp.float32)
        for buf in (own, other):
            buf[pl.ds(NT * ROWS + v * CELLS, 8), :] = const
            buf[pl.ds(NT * ROWS + v * CELLS + 8, 8), :] = const
        for buf in (pit_lo, pit_hi, spa_lo, spa_hi):
            buf[pl.ds(NT * GROWS + v * 8, 8), :] = const
        for buf in (lam, other_lam):
            buf[pl.ds(NT * ROWS + v * CELLS, 8), :] = zero8
            buf[pl.ds(NT * ROWS + v * CELLS + 8, 8), :] = zero8

    def own_loop(p, c):
        for v in range(NV):
            for s in range(4):
                x = own[pl.ds(v * CELLS + p * 4 + s, 8, stride=ROWS), :]
                upad[v, p + 2, s + 2] = x
                buf = send_lo if s < 2 else send_hi
                buf[pl.ds(v * 8 + p * 2 + s % 2, 8, stride=GROWS), :] = x
        return c

    lax.fori_loop(0, 4, own_loop, 0)

    count = jnp.int32(3) + jnp.where(first, 0, 1) + jnp.where(last, 0, 1)
    pl.semaphore_wait(bar, count)

    def remote(k, src, dst, who):
        return pltpu.make_async_remote_copy(
            src_ref=src, dst_ref=dst, send_sem=send_sem.at[k], recv_sem=recv_sem.at[k],
            device_id=who, device_id_type=MESH)

    live = pl.ds(0, NT * GROWS)
    own3 = own
    c_rstate = remote(0, own.at[pl.ds(0, NT * ROWS)], other.at[pl.ds(0, NT * ROWS)], mate)
    c_rlam = remote(1, lam.at[pl.ds(0, NT * ROWS)], other_lam.at[pl.ds(0, NT * ROWS)], mate)
    c_rdis = remote(2, dis.at[pl.ds(32, 16)], other_dis, mate)
    st3 = state.reshape(NT * NV, CELLS, lanes)
    c_pup = remote(3, st3.at[:, pl.ds(8, 8), :], pit_lo.reshape(8 * NV, 8, lanes).at[pl.ds(0, NT * NV)], right)
    c_pdn = remote(4, st3.at[:, pl.ds(0, 8), :], pit_hi.reshape(8 * NV, 8, lanes).at[pl.ds(0, NT * NV)], left)
    c_dpup = remote(5, dis.at[pl.ds(8, 8)], dpit_lo, right)
    c_dpdn = remote(6, dis.at[pl.ds(0, 8)], dpit_hi, left)
    c_sup = remote(7, send_hi.at[live], spa_lo.at[live], upper)
    c_sdn = remote(8, send_lo.at[live], spa_hi.at[live], lower)
    c_dsup = remote(9, dis.at[pl.ds(16, 16)], dspa_lo, upper)
    c_dsdn = remote(10, dis.at[pl.ds(16, 16)], dspa_hi, lower)

    c_pup.start()
    c_pdn.start()
    c_rstate.start()
    loads[2].wait()
    c_dpup.start()
    c_dpdn.start()
    c_rdis.start()

    @pl.when(jnp.logical_not(first))
    def _():
        c_sdn.start()
        c_dsdn.start()

    @pl.when(jnp.logical_not(last))
    def _():
        c_sup.start()
        c_dsup.start()

    loads[0].wait()
    c_rlam.start()

    coup = coupling_matrix()

    def w_loop(j, c):
        base = pl.multiple_of(j * 8, 8)
        rows = [lam[pl.ds(n * ROWS + base, 8), :] for n in range(NT)]
        for m in range(NT):
            t = None
            for n in range(NT):
                if n != m:
                    x = coup[n][m] * rows[n]
                    t = x if t is None else t + x
            wbuf[pl.ds(m * ROWS + base, 8), :] = t
        wbuf[pl.ds(NT * ROWS + base, 8), :] = zero8
        return c

    lax.fori_loop(0, ROWS // 8, w_loop, 0)

    def z_loop(i, c):
        for v in range(NV):
            for j in range(8):
                acc[v, i, j] = zero8
        return c

    lax.fori_loop(0, 8, z_loop, 0)
    for k in range(24):
        cP[k] = zero8
        cS[k] = zero8

    lane = lax.broadcasted_iota(jnp.int32, (8, lanes), 1)
    lane0 = lane == 0
    lane_last = lane == lanes - 1
    low2 = lane < 2
    high2 = lane >= lanes - 2
    one = jnp.where(core0, lanes - 1, 1)
    three = jnp.where(core0, lanes - 3, 3)
    cell = jnp.where(core0, lane, lanes - 1 - lane)
    from_mate = cell >= lanes - 2
    ghost_mate = cell < 2
    ends = jnp.logical_or(lane0, lane_last)

    def ghost(x, y):
        return jnp.where(ghost_mate, y, jnp.where(ends, pltpu.roll(x, one, 1), pltpu.roll(x, three, 1)))

    def unghost(g):
        return jnp.where(cell == 0, pltpu.roll(g, lanes - one, 1),
                         jnp.where(cell == 1, pltpu.roll(g, lanes - three, 1), 0.0))

    def up1(x, g):
        return pltpu.roll(jnp.where(lane0, g, x), lanes - 1, 1)

    def up2(x, g):
        return pltpu.roll(jnp.where(low2, g, x), lanes - 2, 1)

    def dn1(x, g):
        return pltpu.roll(jnp.where(lane_last, g, x), 1, 1)

    def back(cm, c0, c1, c2):
        x, g = c0, None
        for c, amount, mask in ((cm, lanes - 1, lane_last), (c1, 1, lane0), (c2, 2, low2)):
            if c is None:
                continue
            z = pltpu.roll(c, amount, 1)
            part = jnp.where(mask, 0.0, z)
            gpart = jnp.where(mask, z, 0.0)
            x = part if x is None else x + part
            g = gpart if g is None else g + gpart
        return x, g

    def wide(ref, i):
        return jnp.broadcast_to(ref[pl.ds(i, 1), :], (8, lanes))

    def lam_at(i, v):
        return lam[pl.ds(v * CELLS + i, 8, stride=ROWS), :]

    c_rstate.wait_recv()
    c_rdis.wait_recv()
    c_rlam.wait_recv()

    def rad_loop(i, carry):
        p, s = i // 4, i % 4
        x = [upad[v, p + 2, s + 2] for v in range(NV)]
        g = [ghost(x[v], other[pl.ds(v * CELLS + i, 8, stride=ROWS), :]) for v in range(NV)]
        for v in range(NV):
            gho[v, i] = g[v]
        sh = wide(dis, 32 + i)
        shg = ghost(sh, wide(other_dis, i))
        dG[i] = shg
        cot, wallcot = [], []
        for v in range(NV):
            a = lam_at(i, v)
            y = other_lam[pl.ds(v * CELLS + i, 8, stride=ROWS), :]
            y = jnp.where(core0, y, 0.0)
            cot.append(a - up1(a, y))
            wallcot.append(jnp.where(jnp.logical_and(core0, lane0), -a, 0.0))
        cells = [[dn1(x[v], g[v]) for v in range(NV)], x,
                 [up1(x[v], g[v]) for v in range(NV)], [up2(x[v], g[v]) for v in range(NV)]]

        def f(cells, s1, s2):
            o, w = faces(2, cells, {1: s1, 2: s2})
            return o[0], w

        _, pull = jax.vjp(f, cells, sh, up1(sh, shg))
        bar_cells, b1, b2 = pull((cot, wallcot))
        for v in range(NV):
            xb, gb = back(bar_cells[0][v], bar_cells[1][v], bar_cells[2][v], bar_cells[3][v])
            acc[v, p + 2, s + 2] = xb
            gacc[v, i] = gb
        xb, gb = back(None, b1, b2, None)
        cR[i] = xb
        cG[i] = gb
        return carry

    lax.fori_loop(0, CELLS, rad_loop, 0)

    @pl.when(first)
    def _():
        def body(p, c):
            for v in range(NV):
                upad[v, p + 2, 1] = upad[v, p + 2, 2]
                upad[v, p + 2, 0] = upad[v, p + 2, 3]
            dS[pl.ds(p, 1), :] = dis[pl.ds(16 + p * 4, 1), :]
            return c
        lax.fori_loop(0, 4, body, 0)

    @pl.when(jnp.logical_not(first))
    def _():
        c_sup.wait_recv()
        c_dsup.wait_recv()

        def body(p, c):
            for v in range(NV):
                for s in range(2):
                    upad[v, p + 2, s] = spa_lo[pl.ds(v * 8 + p * 2 + s, 8, stride=GROWS), :]
            dS[pl.ds(p, 1), :] = dspa_lo[pl.ds(p * 4 + 3, 1), :]
            return c
        lax.fori_loop(0, 4, body, 0)

    @pl.when(last)
    def _():
        def body(p, c):
            for v in range(NV):
                upad[v, p + 2, 6] = upad[v, p + 2, 5]
                upad[v, p + 2, 7] = upad[v, p + 2, 4]
            dS[pl.ds(20 + p, 1), :] = dis[pl.ds(16 + p * 4 + 3, 1), :]
            return c
        lax.fori_loop(0, 4, body, 0)

    @pl.when(jnp.logical_not(last))
    def _():
        c_sdn.wait_recv()
        c_dsdn.wait_recv()

        def body(p, c):
            for v in range(NV):
                for s in range(2):
                    upad[v, p + 2, 6 + s] = spa_hi[pl.ds(v * 8 + p * 2 + s, 8, stride=GROWS), :]
            dS[pl.ds(20 + p, 1), :] = dspa_hi[pl.ds(p * 4, 1), :]
            return c
        lax.fori_loop(0, 4, body, 0)

    for k in range(4):
        for p in range(4):
            dS[pl.ds((k + 1) * 4 + p, 1), :] = dis[pl.ds(16 + p * 4 + k, 1), :]
            dP[pl.ds((k + 1) * 4 + p, 1), :] = dis[pl.ds(k * 4 + p, 1), :]

    def line(d, cells, shift, lams):
        cot = []
        for i in range(1, 6):
            row = []
            for v in range(NV):
                if i == 1:
                    row.append(-lams[0][v])
                elif i == 5:
                    row.append(lams[3][v])
                else:
                    row.append(lams[i - 2][v] - lams[i - 1][v])
            cot.append(row)
        _, pull = jax.vjp(lambda c, s: faces(d, c, dict(zip(range(1, 7), s)))[0], cells, shift)
        return pull(cot)

    def span_loop(p, carry):
        cells = [[upad[v, p + 2, k] for v in range(NV)] for k in range(8)]
        shift = [wide(dS, k * 4 + p) for k in range(6)]
        lams = [[lam_at(p * 4 + k, v) for v in range(NV)] for k in range(4)]
        bc, bs = line(1, cells, shift, lams)
        for k in range(8):
            for v in range(NV):
                acc[v, p + 2, k] += bc[k][v]
        for k in range(6):
            cS[k * 4 + p] += bs[k]
        return carry

    lax.fori_loop(0, 4, span_loop, 0)

    c_pup.wait_recv()
    c_dpup.wait_recv()
    c_pdn.wait_recv()
    c_dpdn.wait_recv()

    def pit_ghosts(s, c):
        for v in range(NV):
            for k in range(2):
                upad[v, k, s + 2] = pit_lo[pl.ds(v * 8 + k * 4 + s, 8, stride=GROWS), :]
                upad[v, 6 + k, s + 2] = pit_hi[pl.ds(v * 8 + k * 4 + s, 8, stride=GROWS), :]
        dP[pl.ds(s, 1), :] = dpit_lo[pl.ds(4 + s, 1), :]
        dP[pl.ds(20 + s, 1), :] = dpit_hi[pl.ds(s, 1), :]
        return c

    lax.fori_loop(0, 4, pit_ghosts, 0)

    def pitch_loop(s, carry):
        cells = [[upad[v, k, s + 2] for v in range(NV)] for k in range(8)]
        shift = [wide(dP, k * 4 + s) for k in range(6)]
        lams = [[lam_at(k * 4 + s, v) for v in range(NV)] for k in range(4)]
        bc, bs = line(0, cells, shift, lams)
        for k in range(8):
            for v in range(NV):
                acc[v, k, s + 2] += bc[k][v]
        for k in range(6):
            cP[k * 4 + s] += bs[k]
        return carry

    lax.fori_loop(0, 4, pitch_loop, 0)

    pos = (ir * lanes + lane).astype(jnp.float32) + 0.5
    inv_wall = 1.0 / jnp.minimum(pos, n_rad * lanes - pos)

    def cell_loop(i, carry):
        p, s = i // 4, i % 4
        a, b = p + 2, s + 2
        x = [upad[v, a, b] for v in range(NV)]
        g = [gho[v, i] for v in range(3)]
        pu = [upad[v, a + 1, b] for v in (0, 2, 3)]
        pd = [upad[v, a - 1, b] for v in (0, 2, 3)]
        su = [upad[v, a, b + 1] for v in (0, 1, 3)]
        sd = [upad[v, a, b - 1] for v in (0, 1, 3)]
        ru = [up1(x[v], g[v]) for v in (0, 1, 2)]
        rd = [dn1(x[v], g[v]) for v in (0, 1, 2)]
        _, pull = jax.vjp(lambda *t: source(*t, inv_wall), pu, pd, su, sd, ru, rd, x[0], x[5])
        bpu, bpd, bsu, bsd, bru, brd, brho, bnu = pull(lam_at(i, 5))
        for j, v in enumerate((0, 2, 3)):
            acc[v, a + 1, b] += bpu[j]
            acc[v, a - 1, b] += bpd[j]
        for j, v in enumerate((0, 1, 3)):
            acc[v, a, b + 1] += bsu[j]
            acc[v, a, b - 1] += bsd[j]
        extra = [brho, None, None, None, None, bnu]
        for j, v in enumerate((0, 1, 2)):
            xb, gb = back(brd[j], extra[v], bru[j], None)
            extra[v] = xb
            gacc[v, i] += gb
        dpu, dpd = wide(dP, (p + 2) * 4 + s), wide(dP, p * 4 + s)
        dsu, dsd = wide(dS, (s + 2) * 4 + p), wide(dS, s * 4 + p)
        sh, shg = wide(dis, 32 + i), dG[i]
        f0 = 1.0 + 0.5 * (dpu - dpd)
        f1 = 1.0 + 0.5 * (dsu - dsd)
        f2 = 1.0 + 0.5 * (up1(sh, shg) - dn1(sh, shg))
        f01 = f0 * f1
        vol = FREQUENCY * f01 * f2
        vbar = None
        for v in range(NV):
            w = wbuf[pl.ds(v * CELLS + i, 8, stride=ROWS), :]
            t = vol * w
            if extra[v] is not None:
                t = t + extra[v]
            acc[v, a, b] += t
            vbar = w * x[v] if vbar is None else vbar + w * x[v]
        h = (0.5 * FREQUENCY) * vbar
        h0 = h * (f1 * f2)
        h1 = h * (f0 * f2)
        h2 = h * f01
        cP[(p + 2) * 4 + s] += h0
        cP[p * 4 + s] -= h0
        cS[(s + 2) * 4 + p] += h1
        cS[s * 4 + p] -= h1
        xb, gb = back(-h2, None, h2, None)
        cR[i] += xb
        cG[i] += gb
        return carry

    lax.fori_loop(0, CELLS, cell_loop, 0)

    def total(x):
        return jnp.sum(x, axis=0, keepdims=True)

    gone = NT * GROWS + 8
    sent = pl.ds(0, gone)

    def pit_pack(s, c):
        for v in range(NV):
            for k in range(2):
                rp_send_lo[pl.ds(v * 8 + k * 4 + s, 8, stride=GROWS), :] = acc[v, k, s + 2]
                rp_send_hi[pl.ds(v * 8 + k * 4 + s, 8, stride=GROWS), :] = acc[v, 6 + k, s + 2]
        return c

    lax.fori_loop(0, 4, pit_pack, 0)
    for buf in (rp_send_lo, rp_send_hi):
        buf[pl.ds(NT * GROWS, 8), :] = zero8
    for s in range(4):
        rp_send_lo[pl.ds(NT * GROWS + s, 1), :] = total(cP[s])
        rp_send_hi[pl.ds(NT * GROWS + s, 1), :] = total(cP[20 + s])
    r_pup = remote(11, rp_send_hi.at[sent], rp_lo.at[sent], right)
    r_pdn = remote(12, rp_send_lo.at[sent], rp_hi.at[sent], left)
    r_pup.start()
    r_pdn.start()

    def spa_pack(p, c):
        for v in range(NV):
            for k in range(2):
                rs_send_lo[pl.ds(v * 8 + p * 2 + k, 8, stride=GROWS), :] = acc[v, p + 2, k]
                rs_send_hi[pl.ds(v * 8 + p * 2 + k, 8, stride=GROWS), :] = acc[v, p + 2, 6 + k]
        return c

    lax.fori_loop(0, 4, spa_pack, 0)
    for buf in (rs_send_lo, rs_send_hi):
        buf[pl.ds(NT * GROWS, 8), :] = zero8
    for p in range(4):
        rs_send_lo[pl.ds(NT * GROWS + p, 1), :] = total(cS[p])
        rs_send_hi[pl.ds(NT * GROWS + p, 1), :] = total(cS[20 + p])
    r_sup = remote(13, rs_send_hi.at[sent], rs_lo.at[sent], upper)
    r_sdn = remote(14, rs_send_lo.at[sent], rs_hi.at[sent], lower)

    @pl.when(jnp.logical_not(first))
    def _():
        r_sdn.start()

    @pl.when(jnp.logical_not(last))
    def _():
        r_sup.start()

    for i in range(CELLS):
        rr_dsend[pl.ds(i, 1), :] = total(cG[i])
    r_rad = remote(15, gacc, rr_recv, mate)
    r_rdis = remote(16, rr_dsend, rr_drecv, mate)
    r_rad.start()
    r_rdis.start()

    for p in range(4):
        for s in range(4):
            out_disp[pl.ds(p * 4 + s, 1), :] = total(cP[(p + 1) * 4 + s])
            out_disp[pl.ds(16 + p * 4 + s, 1), :] = total(cS[(s + 1) * 4 + p])
            out_disp[pl.ds(32 + p * 4 + s, 1), :] = total(cR[p * 4 + s] + unghost(cG[p * 4 + s]))

    @pl.when(first)
    def _():
        def body(p, c):
            for v in range(NV):
                acc[v, p + 2, 2] += acc[v, p + 2, 1]
                acc[v, p + 2, 3] += acc[v, p + 2, 0]
            out_disp[pl.ds(16 + p * 4, 1), :] += rs_send_lo[pl.ds(NT * GROWS + p, 1), :]
            return c
        lax.fori_loop(0, 4, body, 0)

    @pl.when(last)
    def _():
        def body(p, c):
            for v in range(NV):
                acc[v, p + 2, 5] += acc[v, p + 2, 6]
                acc[v, p + 2, 4] += acc[v, p + 2, 7]
            out_disp[pl.ds(16 + p * 4 + 3, 1), :] += rs_send_hi[pl.ds(NT * GROWS + p, 1), :]
            return c
        lax.fori_loop(0, 4, body, 0)

    r_rad.wait_recv()
    r_rdis.wait_recv()

    def rad_finish(i, c):
        p, s = i // 4, i % 4
        for v in range(NV):
            acc[v, p + 2, s + 2] += unghost(gacc[v, i]) + jnp.where(from_mate, rr_recv[v, i], 0.0)
        return c

    lax.fori_loop(0, CELLS, rad_finish, 0)
    for j in range(2):
        out_disp[pl.ds(32 + 8 * j, 8), :] += jnp.where(from_mate, rr_drecv[pl.ds(8 * j, 8), :], 0.0)

    @pl.when(jnp.logical_not(first))
    def _():
        r_sup.wait_recv()

        def body(p, c):
            for v in range(NV):
                for k in range(2):
                    acc[v, p + 2, 2 + k] += rs_lo[pl.ds(v * 8 + p * 2 + k, 8, stride=GROWS), :]
            out_disp[pl.ds(16 + p * 4, 1), :] += rs_lo[pl.ds(NT * GROWS + p, 1), :]
            return c
        lax.fori_loop(0, 4, body, 0)

    @pl.when(jnp.logical_not(last))
    def _():
        r_sdn.wait_recv()

        def body(p, c):
            for v in range(NV):
                for k in range(2):
                    acc[v, p + 2, 4 + k] += rs_hi[pl.ds(v * 8 + p * 2 + k, 8, stride=GROWS), :]
            out_disp[pl.ds(16 + p * 4 + 3, 1), :] += rs_hi[pl.ds(NT * GROWS + p, 1), :]
            return c
        lax.fori_loop(0, 4, body, 0)

    r_pup.wait_recv()
    r_pdn.wait_recv()

    def finish(s, c):
        for v in range(NV):
            for p in range(4):
                buf = rp_lo if p < 2 else rp_hi
                x = acc[v, p + 2, s + 2] + buf[pl.ds(v * 8 + (p % 2) * 4 + s, 8, stride=GROWS), :]
                out_state[pl.ds(v * CELLS + p * 4 + s, NT, stride=ROWS), :] = x[:NT]
        out_disp[pl.ds(s, 1), :] += rp_lo[pl.ds(NT * GROWS + s, 1), :]
        out_disp[pl.ds(12 + s, 1), :] += rp_hi[pl.ds(NT * GROWS + s, 1), :]
        return c

    lax.fori_loop(0, 4, finish, 0)

    for c in (c_rstate, c_rlam, c_rdis, c_pup, c_pdn, c_dpup, c_dpdn, r_pup, r_pdn, r_rad, r_rdis):
        c.wait_send()

    @pl.when(jnp.logical_not(first))
    def _():
        for c in (c_sdn, c_dsdn, r_sdn):
            c.wait_send()

    @pl.when(jnp.logical_not(last))
    def _():
        for c in (c_sup, c_dsup, r_sup):
            c.wait_send()


def solution(mesh):
    def body(state, adjoint, displacement):
        lanes = state.shape[-1]
        sizes = (mesh.shape["pitch"], mesh.shape["span"], mesh.shape["radial"], lanes)
        f32 = jnp.float32

        def vm(*lead):
            return pltpu.VMEM(tuple(lead) + (lanes,), f32)

        scratch = [
            vm(8 * ROWS), vm(8 * ROWS), vm(48), vm(8 * ROWS), vm(8 * ROWS), vm(16),
            vm(8 * GROWS), vm(8 * GROWS), vm(8 * GROWS), vm(8 * GROWS), vm(8), vm(8), vm(16), vm(16),
            vm(8 * GROWS), vm(8 * GROWS),
            vm(NV, 8, 8, 8), vm(NV, 8, 8, 8), vm(NV, CELLS, 8), vm(NV, CELLS, 8), vm(8 * ROWS),
            vm(24), vm(24), vm(16), vm(16, 8), vm(24, 8), vm(24, 8), vm(16, 8), vm(16, 8),
            vm(8 * GROWS), vm(8 * GROWS), vm(8 * GROWS), vm(8 * GROWS),
            vm(8 * GROWS), vm(8 * GROWS), vm(8 * GROWS), vm(8 * GROWS),
            vm(NV, CELLS, 8), vm(16), vm(16),
            pltpu.SemaphoreType.DMA((3,)), pltpu.SemaphoreType.DMA((17,)), pltpu.SemaphoreType.DMA((17,)),
        ]
        any_spec = pl.BlockSpec(memory_space=pl.ANY)
        vmem_spec = pl.BlockSpec(memory_space=pltpu.VMEM)
        out_state, out_disp = pl.pallas_call(
            lambda *refs: kernel(sizes, *refs),
            out_shape=(
                jax.ShapeDtypeStruct((NT * ROWS, lanes), f32),
                jax.ShapeDtypeStruct((3 * CELLS, lanes), f32),
            ),
            in_specs=[any_spec] * 3,
            out_specs=(vmem_spec, vmem_spec),
            scratch_shapes=scratch,
            compiler_params=pltpu.CompilerParams(
                collective_id=0, has_side_effects=True, vmem_limit_bytes=40 * 1024 * 1024),
            name="adjoint",
        )(
            state.reshape(NT * ROWS, lanes),
            adjoint.reshape(NT * ROWS, lanes),
            displacement.reshape(3 * CELLS, lanes),
        )
        return out_state.reshape(state.shape), out_disp.reshape(displacement.shape)

    spec = P("group", None, "pitch", "span", "radial")
    dspec = P("group", "pitch", "span", "radial")
    return jax.shard_map(
        body, mesh=mesh, in_specs=(spec, spec, dspec), out_specs=(spec, dspec), check_vma=False)
```

```python
import math

import jax
import jax.numpy as jnp
from jax import lax
from jax.experimental import pallas as pl
from jax.experimental.pallas import tpu as pltpu
from jax.sharding import PartitionSpec as P

NT = 7
NV = 6
LAMINAR_MU = 0.02
CV_CUBE = 7.1**3
SECOND_COEFF = 0.5
FOURTH_COEFF = 1.0 / 32.0
HEAT_DIFFUSIVE = 4.86
SIGMA_TURB = 2.0 / 3.0
PRODUCTION_COEF = 0.1355
CW_ONE = 3.24
FREQUENCY = 1.0
MESH = pl.DeviceIdType.MESH

CELLS = 16
ROWS = NV * CELLS
GROWS = NV * 8
HROWS = NV * 4
PAD_STATE = (1.0, 0.0, 0.0, 0.0, 2.5, 0.1)


def coupling_matrix():
    out = [[0.0] * NT for _ in range(NT)]
    for n in range(NT):
        for m in range(NT):
            if n != m:
                out[n][m] = 0.5 * (-1.0) ** (n - m) / math.sin(math.pi * (n - m) / NT)
    return out


@jax.custom_jvp
def recip(x):
    return 1.0 / x


@recip.defjvp
def recip_jvp(primals, tangents):
    r = recip(primals[0])
    return r, -(r * r) * tangents[0]


@jax.custom_jvp
def root(x):
    return x * lax.rsqrt(x)


@root.defjvp
def root_jvp(primals, tangents):
    x = primals[0]
    y = lax.rsqrt(x)
    return x * y, (0.5 * y) * tangents[0]


def prim(u):
    inv = recip(u[0])
    vel = [u[1] * inv, u[2] * inv, u[3] * inv]
    kin = u[1] * vel[0] + u[2] * vel[1] + u[3] * vel[2]
    return inv, vel, 0.4 * (u[4] - 0.5 * kin)


def faces(d, cells, shift):
    n = len(cells)
    base = [prim(u) for u in cells]
    p = [b[2] for b in base]
    q = {}
    for i in range(1, n - 1):
        u = cells[i]
        inv, vel, pres = base[i]
        temp = pres * inv
        rn = u[0] * u[5]
        ratio = rn * (1.0 / LAMINAR_MU)
        cube = ratio * ratio * ratio
        visc = LAMINAR_MU + rn * (cube * recip(cube + CV_CUBE))
        un = vel[d]
        flux = [un * u[v] for v in range(NV)]
        flux[1 + d] = flux[1 + d] + pres
        flux[4] = flux[4] + pres * un
        radius = root(un * un + 0.01) + root(1.4 * temp)
        square = vel[0] * vel[0] + vel[1] * vel[1] + vel[2] * vel[2]
        ends = p[i + 1] + p[i - 1]
        ratio_p = (ends - 2.0 * pres) * recip(ends + 2.0 * pres)
        q[i] = (vel, temp, rn, visc, flux, radius, 0.5 * square + HEAT_DIFFUSIVE * temp, ratio_p * ratio_p)
    out = []
    for a in range(1, n - 2):
        b = a + 1
        qa, qb = q[a], q[b]
        eps_two = SECOND_COEFF * 0.5 * (qa[7] + qb[7])
        eps_four = FOURTH_COEFF * FOURTH_COEFF * recip(FOURTH_COEFF + eps_two)
        spread = 0.5 * (qa[5] + qb[5])
        two, four = spread * eps_two, spread * eps_four
        isp = recip(1.0 + shift[b] - shift[a])
        mu = 0.5 * (qa[3] + qb[3]) * isp
        turb = (LAMINAR_MU + 0.5 * (qa[2] + qb[2])) * (1.0 / SIGMA_TURB) * isp
        face = []
        for v in range(NV):
            jump = cells[b][v] - cells[a][v]
            third = cells[b + 1][v] - cells[a - 1][v] - 3.0 * jump
            f = 0.5 * (qa[4][v] + qb[4][v]) - two * jump + four * third
            if 1 <= v <= 3:
                f = f - mu * (qb[0][v - 1] - qa[0][v - 1])
            elif v == 4:
                f = f - mu * (qb[6] - qa[6])
            elif v == 5:
                f = f - turb * jump
            face.append(f)
        out.append(face)
    return out, q[1][4]


def source(pitch_up, pitch_dn, span_up, span_dn, rad_up, rad_dn, rho, nu, inv_wall):
    def gap(up, dn, k):
        return 0.5 * (up[k] * recip(up[0]) - dn[k] * recip(dn[0]))

    cx = gap(span_up, span_dn, 2) - gap(rad_up, rad_dn, 2)
    cy = gap(rad_up, rad_dn, 1) - gap(pitch_up, pitch_dn, 2)
    cz = gap(pitch_up, pitch_dn, 1) - gap(span_up, span_dn, 1)
    vort = root(cx * cx + cy * cy + cz * cz + 0.01)
    scaled = nu * inv_wall
    return rho * (CW_ONE * scaled * scaled - PRODUCTION_COEF * vort * nu)


def kernel(sizes, state, adjoint, disp, out_state, out_disp,
           own, lam, dis, other, other_lam, other_dis,
           pit_lo, pit_hi, spa_lo, spa_hi, dpit_lo, dpit_hi, dspa_lo, dspa_hi,
           send_lo, send_hi, psend_lo, psend_hi,
           upad, acc, gho, gacc, wbuf, dP, dS, dR, dG, cP, cS, cR, cG,
           rp_send_lo, rp_send_hi, rp_lo, rp_hi, rs_send_lo, rs_send_hi, rs_lo, rs_hi,
           rr_recv, rr_dsend, rr_drecv,
           local_sem, send_sem, recv_sem):
    n_pitch, n_span, n_rad, lanes = sizes
    ip = lax.axis_index("pitch")
    isp = lax.axis_index("span")
    ir = lax.axis_index("radial")
    ig = lax.axis_index("group")
    left = (ig, lax.rem(ip + n_pitch - 1, n_pitch), isp, ir)
    right = (ig, lax.rem(ip + 1, n_pitch), isp, ir)
    lower = (ig, ip, lax.rem(isp + n_span - 1, n_span), ir)
    upper = (ig, ip, lax.rem(isp + 1, n_span), ir)
    mate = (ig, ip, isp, 1 - ir)
    first = isp == 0
    last = isp == n_span - 1
    core0 = ir == 0

    loads = [
        pltpu.make_async_copy(adjoint, lam.at[pl.ds(0, NT * ROWS)], local_sem.at[1]),
        pltpu.make_async_copy(state, own.at[pl.ds(0, NT * ROWS)], local_sem.at[0]),
        pltpu.make_async_copy(disp, dis, local_sem.at[2]),
    ]
    for c in loads:
        c.start()

    bar = pltpu.get_barrier_semaphore()
    for who in (left, right, mate):
        pl.semaphore_signal(bar, inc=1, device_id=who, device_id_type=MESH)

    @pl.when(jnp.logical_not(first))
    def _():
        pl.semaphore_signal(bar, inc=1, device_id=lower, device_id_type=MESH)

    @pl.when(jnp.logical_not(last))
    def _():
        pl.semaphore_signal(bar, inc=1, device_id=upper, device_id_type=MESH)

    loads[1].wait()
    zero8 = jnp.zeros((8, lanes), jnp.float32)
    for v in range(NV):
        const = jnp.full((8, lanes), PAD_STATE[v], jnp.float32)
        for buf in (own, other):
            buf[pl.ds(NT * ROWS + v * CELLS, 8), :] = const
            buf[pl.ds(NT * ROWS + v * CELLS + 8, 8), :] = const
        for buf in (spa_lo, spa_hi):
            buf[pl.ds(NT * GROWS + v * 8, 8), :] = const
        for buf in (lam, other_lam):
            buf[pl.ds(NT * ROWS + v * CELLS, 8), :] = zero8
            buf[pl.ds(NT * ROWS + v * CELLS + 8, 8), :] = zero8

    sub = lax.broadcasted_iota(jnp.int32, (8, lanes), 0)
    for v in range(0, NV, 2):
        const = jnp.where(sub < 4, PAD_STATE[v], PAD_STATE[v + 1])
        for buf in (pit_lo, pit_hi):
            for h in range(2):
                buf[pl.ds(h * 8 * HROWS + NT * HROWS + v * 4, 8), :] = const

    for p in range(4):
        for s in range(4):
            h, s2 = s // 2, s % 2
            for v in range(NV):
                x = own[pl.ds(v * CELLS + p * 4 + s, 8, stride=ROWS), :]
                upad[v, p + 2, s + 2] = x
                buf = send_lo if s < 2 else send_hi
                buf[pl.ds(v * 8 + p * 2 + s2, 8, stride=GROWS), :] = x
                buf = psend_lo if p < 2 else psend_hi
                buf[pl.ds(h * 8 * HROWS + v * 4 + (p % 2) * 2 + s2, 8, stride=HROWS), :] = x

    count = jnp.int32(3) + jnp.where(first, 0, 1) + jnp.where(last, 0, 1)
    pl.semaphore_wait(bar, count)

    def remote(k, src, dst, who):
        return pltpu.make_async_remote_copy(
            src_ref=src, dst_ref=dst, send_sem=send_sem.at[k], recv_sem=recv_sem.at[k],
            device_id=who, device_id_type=MESH)

    live = pl.ds(0, NT * GROWS)
    c_rstate = remote(0, own.at[pl.ds(0, NT * ROWS)], other.at[pl.ds(0, NT * ROWS)], mate)
    c_rlam = remote(1, lam.at[pl.ds(0, NT * ROWS)], other_lam.at[pl.ds(0, NT * ROWS)], mate)
    c_rdis = remote(2, dis.at[pl.ds(32, 16)], other_dis, mate)
    part = [pl.ds(h * 8 * HROWS, NT * HROWS) for h in range(2)]
    c_pup = [remote((3, 17)[h], psend_hi.at[part[h]], pit_lo.at[part[h]], right) for h in range(2)]
    c_pdn = [remote((4, 18)[h], psend_lo.at[part[h]], pit_hi.at[part[h]], left) for h in range(2)]
    c_dpup = remote(5, dis.at[pl.ds(8, 8)], dpit_lo, right)
    c_dpdn = remote(6, dis.at[pl.ds(0, 8)], dpit_hi, left)
    c_sup = remote(7, send_hi.at[live], spa_lo.at[live], upper)
    c_sdn = remote(8, send_lo.at[live], spa_hi.at[live], lower)
    c_dsup = remote(9, dis.at[pl.ds(16, 16)], dspa_lo, upper)
    c_dsdn = remote(10, dis.at[pl.ds(16, 16)], dspa_hi, lower)

    loads[2].wait()
    c_dpup.start()
    c_dpdn.start()
    c_pup[0].start()
    c_pdn[0].start()
    c_rstate.start()
    c_rdis.start()

    @pl.when(jnp.logical_not(first))
    def _():
        c_sdn.start()
        c_dsdn.start()

    @pl.when(jnp.logical_not(last))
    def _():
        c_sup.start()
        c_dsup.start()

    c_pup[1].start()
    c_pdn[1].start()
    loads[0].wait()
    c_rlam.start()

    coup = coupling_matrix()

    def w_loop(j, c):
        base = pl.multiple_of(j * 8, 8)
        rows = [lam[pl.ds(n * ROWS + base, 8), :] for n in range(NT)]
        for m in range(NT):
            t = None
            for n in range(NT):
                if n != m:
                    x = coup[n][m] * rows[n]
                    t = x if t is None else t + x
            wbuf[pl.ds(m * ROWS + base, 8), :] = t
        wbuf[pl.ds(NT * ROWS + base, 8), :] = zero8
        return c

    lax.fori_loop(0, ROWS // 8, w_loop, 0)

    def z_loop(i, c):
        for v in range(NV):
            for j in range(8):
                acc[v, i, j] = zero8
        return c

    lax.fori_loop(0, 8, z_loop, 0)
    for k in range(24):
        cP[k] = zero8
        cS[k] = zero8

    lane = lax.broadcasted_iota(jnp.int32, (8, lanes), 1)
    lane0 = lane == 0
    lane_last = lane == lanes - 1
    low2 = lane < 2
    high2 = lane >= lanes - 2
    one = jnp.where(core0, lanes - 1, 1)
    three = jnp.where(core0, lanes - 3, 3)
    cell = jnp.where(core0, lane, lanes - 1 - lane)
    from_mate = cell >= lanes - 2
    ghost_mate = cell < 2
    ends = jnp.logical_or(lane0, lane_last)

    def ghost(x, y):
        return jnp.where(ghost_mate, y, jnp.where(ends, pltpu.roll(x, one, 1), pltpu.roll(x, three, 1)))

    def unghost(g):
        return jnp.where(cell == 0, pltpu.roll(g, lanes - one, 1),
                         jnp.where(cell == 1, pltpu.roll(g, lanes - three, 1), 0.0))

    def up1(x, g):
        return pltpu.roll(jnp.where(lane0, g, x), lanes - 1, 1)

    def up2(x, g):
        return pltpu.roll(jnp.where(low2, g, x), lanes - 2, 1)

    def dn1(x, g):
        return pltpu.roll(jnp.where(lane_last, g, x), 1, 1)

    def back(cm, c0, c1, c2):
        x, g = c0, None
        for c, amount, mask in ((cm, lanes - 1, lane_last), (c1, 1, lane0), (c2, 2, low2)):
            if c is None:
                continue
            z = pltpu.roll(c, amount, 1)
            part = jnp.where(mask, 0.0, z)
            gpart = jnp.where(mask, z, 0.0)
            x = part if x is None else x + part
            g = gpart if g is None else g + gpart
        return x, g

    def wide(ref, i):
        return jnp.broadcast_to(ref[pl.ds(i, 1), :], (8, lanes))

    def lam_at(i, v):
        return lam[pl.ds(v * CELLS + i, 8, stride=ROWS), :]

    c_rstate.wait_recv()
    c_rdis.wait_recv()
    c_rlam.wait_recv()

    def rad_loop(i, carry):
        p, s = i // 4, i % 4
        x = [upad[v, p + 2, s + 2] for v in range(NV)]
        g = [ghost(x[v], other[pl.ds(v * CELLS + i, 8, stride=ROWS), :]) for v in range(NV)]
        for v in range(NV):
            gho[v, i] = g[v]
        sh = wide(dis, 32 + i)
        shg = ghost(sh, wide(other_dis, i))
        dG[i] = shg
        cot, wallcot = [], []
        for v in range(NV):
            a = lam_at(i, v)
            y = other_lam[pl.ds(v * CELLS + i, 8, stride=ROWS), :]
            y = jnp.where(core0, y, 0.0)
            cot.append(a - up1(a, y))
            wallcot.append(jnp.where(jnp.logical_and(core0, lane0), -a, 0.0))
        cells = [[dn1(x[v], g[v]) for v in range(NV)], x,
                 [up1(x[v], g[v]) for v in range(NV)], [up2(x[v], g[v]) for v in range(NV)]]

        def f(cells, s1, s2):
            o, w = faces(2, cells, {1: s1, 2: s2})
            return o[0], w

        _, pull = jax.vjp(f, cells, sh, up1(sh, shg))
        bar_cells, b1, b2 = pull((cot, wallcot))
        for v in range(NV):
            xb, gb = back(bar_cells[0][v], bar_cells[1][v], bar_cells[2][v], bar_cells[3][v])
            acc[v, p + 2, s + 2] = xb
            gacc[v, i] = gb
        xb, gb = back(None, b1, b2, None)
        cR[i] = xb
        cG[i] = gb
        return carry

    lax.fori_loop(0, CELLS, rad_loop, 0)

    @pl.when(first)
    def _():
        def body(p, c):
            for v in range(NV):
                upad[v, p + 2, 1] = upad[v, p + 2, 2]
                upad[v, p + 2, 0] = upad[v, p + 2, 3]
            dS[pl.ds(p, 1), :] = dis[pl.ds(16 + p * 4, 1), :]
            return c
        lax.fori_loop(0, 4, body, 0)

    @pl.when(jnp.logical_not(first))
    def _():
        c_sup.wait_recv()
        c_dsup.wait_recv()

        def body(p, c):
            for v in range(NV):
                for s in range(2):
                    upad[v, p + 2, s] = spa_lo[pl.ds(v * 8 + p * 2 + s, 8, stride=GROWS), :]
            dS[pl.ds(p, 1), :] = dspa_lo[pl.ds(p * 4 + 3, 1), :]
            return c
        lax.fori_loop(0, 4, body, 0)

    @pl.when(last)
    def _():
        def body(p, c):
            for v in range(NV):
                upad[v, p + 2, 6] = upad[v, p + 2, 5]
                upad[v, p + 2, 7] = upad[v, p + 2, 4]
            dS[pl.ds(20 + p, 1), :] = dis[pl.ds(16 + p * 4 + 3, 1), :]
            return c
        lax.fori_loop(0, 4, body, 0)

    @pl.when(jnp.logical_not(last))
    def _():
        c_sdn.wait_recv()
        c_dsdn.wait_recv()

        def body(p, c):
            for v in range(NV):
                for s in range(2):
                    upad[v, p + 2, 6 + s] = spa_hi[pl.ds(v * 8 + p * 2 + s, 8, stride=GROWS), :]
            dS[pl.ds(20 + p, 1), :] = dspa_hi[pl.ds(p * 4, 1), :]
            return c
        lax.fori_loop(0, 4, body, 0)

    for k in range(4):
        for p in range(4):
            dS[pl.ds((k + 1) * 4 + p, 1), :] = dis[pl.ds(16 + p * 4 + k, 1), :]
            dP[pl.ds((k + 1) * 4 + p, 1), :] = dis[pl.ds(k * 4 + p, 1), :]

    def line(d, cells, shift, lams):
        cot = []
        for i in range(1, 6):
            row = []
            for v in range(NV):
                if i == 1:
                    row.append(-lams[0][v])
                elif i == 5:
                    row.append(lams[3][v])
                else:
                    row.append(lams[i - 2][v] - lams[i - 1][v])
            cot.append(row)
        _, pull = jax.vjp(lambda c, s: faces(d, c, dict(zip(range(1, 7), s)))[0], cells, shift)
        return pull(cot)

    pos = (ir * lanes + lane).astype(jnp.float32) + 0.5
    inv_wall = 1.0 / jnp.minimum(pos, n_rad * lanes - pos)

    def cell_work(p, s):
        i = p * 4 + s
        a, b = p + 2, s + 2
        x = [upad[v, a, b] for v in range(NV)]
        g = [gho[v, i] for v in range(3)]
        pu = [upad[v, a + 1, b] for v in (0, 2, 3)]
        pd = [upad[v, a - 1, b] for v in (0, 2, 3)]
        su = [upad[v, a, b + 1] for v in (0, 1, 3)]
        sd = [upad[v, a, b - 1] for v in (0, 1, 3)]
        ru = [up1(x[v], g[v]) for v in (0, 1, 2)]
        rd = [dn1(x[v], g[v]) for v in (0, 1, 2)]
        _, pull = jax.vjp(lambda *t: source(*t, inv_wall), pu, pd, su, sd, ru, rd, x[0], x[5])
        bpu, bpd, bsu, bsd, bru, brd, brho, bnu = pull(lam_at(i, 5))
        for j, v in enumerate((0, 2, 3)):
            acc[v, a + 1, b] += bpu[j]
            acc[v, a - 1, b] += bpd[j]
        for j, v in enumerate((0, 1, 3)):
            acc[v, a, b + 1] += bsu[j]
            acc[v, a, b - 1] += bsd[j]
        extra = [brho, None, None, None, None, bnu]
        for j, v in enumerate((0, 1, 2)):
            xb, gb = back(brd[j], extra[v], bru[j], None)
            extra[v] = xb
            gacc[v, i] += gb
        dpu, dpd = wide(dP, (p + 2) * 4 + s), wide(dP, p * 4 + s)
        dsu, dsd = wide(dS, (s + 2) * 4 + p), wide(dS, s * 4 + p)
        sh, shg = wide(dis, 32 + i), dG[i]
        f0 = 1.0 + 0.5 * (dpu - dpd)
        f1 = 1.0 + 0.5 * (dsu - dsd)
        f2 = 1.0 + 0.5 * (up1(sh, shg) - dn1(sh, shg))
        f01 = f0 * f1
        vol = FREQUENCY * f01 * f2
        vbar = None
        for v in range(NV):
            w = wbuf[pl.ds(v * CELLS + i, 8, stride=ROWS), :]
            t = vol * w
            if extra[v] is not None:
                t = t + extra[v]
            acc[v, a, b] += t
            vbar = w * x[v] if vbar is None else vbar + w * x[v]
        h = (0.5 * FREQUENCY) * vbar
        h0 = h * (f1 * f2)
        h1 = h * (f0 * f2)
        h2 = h * f01
        cP[(p + 2) * 4 + s] += h0
        cP[p * 4 + s] -= h0
        cS[(s + 2) * 4 + p] += h1
        cS[s * 4 + p] -= h1
        xb, gb = back(-h2, None, h2, None)
        cR[i] += xb
        cG[i] += gb


    def pitch_line(s):
        cells = [[upad[v, k, s + 2] for v in range(NV)] for k in range(8)]
        shift = [wide(dP, k * 4 + s) for k in range(6)]
        lams = [[lam_at(k * 4 + s, v) for v in range(NV)] for k in range(4)]
        bc, bs = line(0, cells, shift, lams)
        for k in range(8):
            for v in range(NV):
                acc[v, k, s + 2] += bc[k][v]
        for k in range(6):
            cP[k * 4 + s] += bs[k]

    def total(x):
        return jnp.sum(x, axis=0, keepdims=True)

    back_part = [pl.ds(h * 8 * HROWS, NT * HROWS + 8) for h in range(2)]
    r_pup = [remote((11, 19)[h], rp_send_hi.at[back_part[h]], rp_lo.at[back_part[h]], right) for h in range(2)]
    r_pdn = [remote((12, 20)[h], rp_send_lo.at[back_part[h]], rp_hi.at[back_part[h]], left) for h in range(2)]

    def chunk(h):
        c_pup[h].wait_recv()
        c_pdn[h].wait_recv()
        if h == 0:
            c_dpup.wait_recv()
            c_dpdn.wait_recv()
            for s in range(4):
                dP[pl.ds(s, 1), :] = dpit_lo[pl.ds(4 + s, 1), :]
                dP[pl.ds(20 + s, 1), :] = dpit_hi[pl.ds(s, 1), :]

        def ghosts(s2, c):
            s = 2 * h + s2
            for v in range(NV):
                for k in range(2):
                    row = pl.ds(h * 8 * HROWS + v * 4 + k * 2 + s2, 8, stride=HROWS)
                    upad[v, k, s + 2] = pit_lo[row, :]
                    upad[v, 6 + k, s + 2] = pit_hi[row, :]
            pitch_line(s)
            return c

        lax.fori_loop(0, 2, ghosts, 0)

        def cells_loop(j, c):
            cell_work(j // 2, 2 * h + j % 2)
            return c

        lax.fori_loop(0, 8, cells_loop, 0)

        for s2 in range(2):
            s = 2 * h + s2
            for v in range(NV):
                for k in range(2):
                    row = pl.ds(h * 8 * HROWS + v * 4 + k * 2 + s2, 8, stride=HROWS)
                    rp_send_lo[row, :] = acc[v, k, s + 2]
                    rp_send_hi[row, :] = acc[v, 6 + k, s + 2]
        base = h * 8 * HROWS + NT * HROWS
        for buf, k in ((rp_send_lo, 0), (rp_send_hi, 20)):
            buf[pl.ds(base, 8), :] = zero8
            for s2 in range(2):
                buf[pl.ds(base + s2, 1), :] = total(cP[k + 2 * h + s2])
        r_pup[h].start()
        r_pdn[h].start()

    chunk(0)

    def span_loop(p, carry):
        cells = [[upad[v, p + 2, k] for v in range(NV)] for k in range(8)]
        shift = [wide(dS, k * 4 + p) for k in range(6)]
        lams = [[lam_at(p * 4 + k, v) for v in range(NV)] for k in range(4)]
        bc, bs = line(1, cells, shift, lams)
        for k in range(8):
            for v in range(NV):
                acc[v, p + 2, k] += bc[k][v]
        for k in range(6):
            cS[k * 4 + p] += bs[k]
        return carry

    lax.fori_loop(0, 4, span_loop, 0)

    chunk(1)

    gone = NT * GROWS + 8
    sent = pl.ds(0, gone)

    def spa_pack(p, c):
        for v in range(NV):
            for k in range(2):
                rs_send_lo[pl.ds(v * 8 + p * 2 + k, 8, stride=GROWS), :] = acc[v, p + 2, k]
                rs_send_hi[pl.ds(v * 8 + p * 2 + k, 8, stride=GROWS), :] = acc[v, p + 2, 6 + k]
        return c

    lax.fori_loop(0, 4, spa_pack, 0)
    for buf in (rs_send_lo, rs_send_hi):
        buf[pl.ds(NT * GROWS, 8), :] = zero8
    for p in range(4):
        rs_send_lo[pl.ds(NT * GROWS + p, 1), :] = total(cS[p])
        rs_send_hi[pl.ds(NT * GROWS + p, 1), :] = total(cS[20 + p])
    r_sup = remote(13, rs_send_hi.at[sent], rs_lo.at[sent], upper)
    r_sdn = remote(14, rs_send_lo.at[sent], rs_hi.at[sent], lower)

    @pl.when(jnp.logical_not(first))
    def _():
        r_sdn.start()

    @pl.when(jnp.logical_not(last))
    def _():
        r_sup.start()

    for i in range(CELLS):
        rr_dsend[pl.ds(i, 1), :] = total(cG[i])
    r_rad = remote(15, gacc, rr_recv, mate)
    r_rdis = remote(16, rr_dsend, rr_drecv, mate)
    r_rad.start()
    r_rdis.start()

    for p in range(4):
        for s in range(4):
            out_disp[pl.ds(p * 4 + s, 1), :] = total(cP[(p + 1) * 4 + s])
            out_disp[pl.ds(16 + p * 4 + s, 1), :] = total(cS[(s + 1) * 4 + p])
            out_disp[pl.ds(32 + p * 4 + s, 1), :] = total(cR[p * 4 + s] + unghost(cG[p * 4 + s]))

    @pl.when(first)
    def _():
        def body(p, c):
            for v in range(NV):
                acc[v, p + 2, 2] += acc[v, p + 2, 1]
                acc[v, p + 2, 3] += acc[v, p + 2, 0]
            out_disp[pl.ds(16 + p * 4, 1), :] += rs_send_lo[pl.ds(NT * GROWS + p, 1), :]
            return c
        lax.fori_loop(0, 4, body, 0)

    @pl.when(last)
    def _():
        def body(p, c):
            for v in range(NV):
                acc[v, p + 2, 5] += acc[v, p + 2, 6]
                acc[v, p + 2, 4] += acc[v, p + 2, 7]
            out_disp[pl.ds(16 + p * 4 + 3, 1), :] += rs_send_hi[pl.ds(NT * GROWS + p, 1), :]
            return c
        lax.fori_loop(0, 4, body, 0)

    r_rad.wait_recv()
    r_rdis.wait_recv()

    def rad_finish(i, c):
        p, s = i // 4, i % 4
        for v in range(NV):
            acc[v, p + 2, s + 2] += unghost(gacc[v, i]) + jnp.where(from_mate, rr_recv[v, i], 0.0)
        return c

    lax.fori_loop(0, CELLS, rad_finish, 0)
    for j in range(2):
        out_disp[pl.ds(32 + 8 * j, 8), :] += jnp.where(from_mate, rr_drecv[pl.ds(8 * j, 8), :], 0.0)

    @pl.when(jnp.logical_not(first))
    def _():
        r_sup.wait_recv()

        def body(p, c):
            for v in range(NV):
                for k in range(2):
                    acc[v, p + 2, 2 + k] += rs_lo[pl.ds(v * 8 + p * 2 + k, 8, stride=GROWS), :]
            out_disp[pl.ds(16 + p * 4, 1), :] += rs_lo[pl.ds(NT * GROWS + p, 1), :]
            return c
        lax.fori_loop(0, 4, body, 0)

    @pl.when(jnp.logical_not(last))
    def _():
        r_sdn.wait_recv()

        def body(p, c):
            for v in range(NV):
                for k in range(2):
                    acc[v, p + 2, 4 + k] += rs_hi[pl.ds(v * 8 + p * 2 + k, 8, stride=GROWS), :]
            out_disp[pl.ds(16 + p * 4 + 3, 1), :] += rs_hi[pl.ds(NT * GROWS + p, 1), :]
            return c
        lax.fori_loop(0, 4, body, 0)

    for h in range(2):
        r_pup[h].wait_recv()
        r_pdn[h].wait_recv()
        for s2 in range(2):
            s = 2 * h + s2
            for v in range(NV):
                for p in range(4):
                    buf = rp_lo if p < 2 else rp_hi
                    row = pl.ds(h * 8 * HROWS + v * 4 + (p % 2) * 2 + s2, 8, stride=HROWS)
                    x = acc[v, p + 2, s + 2] + buf[row, :]
                    out_state[pl.ds(v * CELLS + p * 4 + s, NT, stride=ROWS), :] = x[:NT]
            row = pl.ds(h * 8 * HROWS + NT * HROWS + s2, 1)
            out_disp[pl.ds(s, 1), :] += rp_lo[row, :]
            out_disp[pl.ds(12 + s, 1), :] += rp_hi[row, :]

    for c in (c_rstate, c_rlam, c_rdis, *c_pup, *c_pdn, c_dpup, c_dpdn, *r_pup, *r_pdn, r_rad, r_rdis):
        c.wait_send()

    @pl.when(jnp.logical_not(first))
    def _():
        for c in (c_sdn, c_dsdn, r_sdn):
            c.wait_send()

    @pl.when(jnp.logical_not(last))
    def _():
        for c in (c_sup, c_dsup, r_sup):
            c.wait_send()


def solution(mesh):
    def body(state, adjoint, displacement):
        lanes = state.shape[-1]
        sizes = (mesh.shape["pitch"], mesh.shape["span"], mesh.shape["radial"], lanes)
        f32 = jnp.float32

        def vm(*lead):
            return pltpu.VMEM(tuple(lead) + (lanes,), f32)

        scratch = [
            vm(8 * ROWS), vm(8 * ROWS), vm(48), vm(8 * ROWS), vm(8 * ROWS), vm(16),
            vm(8 * GROWS), vm(8 * GROWS), vm(8 * GROWS), vm(8 * GROWS), vm(8), vm(8), vm(16), vm(16),
            vm(8 * GROWS), vm(8 * GROWS), vm(8 * GROWS), vm(8 * GROWS),
            vm(NV, 8, 8, 8), vm(NV, 8, 8, 8), vm(NV, CELLS, 8), vm(NV, CELLS, 8), vm(8 * ROWS),
            vm(24), vm(24), vm(16), vm(16, 8), vm(24, 8), vm(24, 8), vm(16, 8), vm(16, 8),
            vm(8 * GROWS), vm(8 * GROWS), vm(8 * GROWS), vm(8 * GROWS),
            vm(8 * GROWS), vm(8 * GROWS), vm(8 * GROWS), vm(8 * GROWS),
            vm(NV, CELLS, 8), vm(16), vm(16),
            pltpu.SemaphoreType.DMA((3,)), pltpu.SemaphoreType.DMA((21,)), pltpu.SemaphoreType.DMA((21,)),
        ]
        any_spec = pl.BlockSpec(memory_space=pl.ANY)
        vmem_spec = pl.BlockSpec(memory_space=pltpu.VMEM)
        out_state, out_disp = pl.pallas_call(
            lambda *refs: kernel(sizes, *refs),
            out_shape=(
                jax.ShapeDtypeStruct((NT * ROWS, lanes), f32),
                jax.ShapeDtypeStruct((3 * CELLS, lanes), f32),
            ),
            in_specs=[any_spec] * 3,
            out_specs=(vmem_spec, vmem_spec),
            scratch_shapes=scratch,
            compiler_params=pltpu.CompilerParams(
                collective_id=0, has_side_effects=True, vmem_limit_bytes=60 * 1024 * 1024),
            name="adjoint",
        )(
            state.reshape(NT * ROWS, lanes),
            adjoint.reshape(NT * ROWS, lanes),
            displacement.reshape(3 * CELLS, lanes),
        )
        return out_state.reshape(state.shape), out_disp.reshape(displacement.shape)

    spec = P("group", None, "pitch", "span", "radial")
    dspec = P("group", "pitch", "span", "radial")
    return jax.shard_map(
        body, mesh=mesh, in_specs=(spec, spec, dspec), out_specs=(spec, dspec), check_vma=False)
```

```python
import math

import jax
import jax.numpy as jnp
from jax import lax
from jax.experimental import pallas as pl
from jax.experimental.pallas import tpu as pltpu
from jax.sharding import PartitionSpec as P

NT = 7
NV = 6
LAMINAR_MU = 0.02
CV_CUBE = 7.1**3
SECOND_COEFF = 0.5
FOURTH_COEFF = 1.0 / 32.0
HEAT_DIFFUSIVE = 4.86
SIGMA_TURB = 2.0 / 3.0
PRODUCTION_COEF = 0.1355
CW_ONE = 3.24
FREQUENCY = 1.0
MESH = pl.DeviceIdType.MESH

CELLS = 16
ROWS = NV * CELLS
GROWS = NV * 8
HROWS = NV * 4
QROWS = NV * 2
PAD_STATE = (1.0, 0.0, 0.0, 0.0, 2.5, 0.1)


def coupling_matrix():
    out = [[0.0] * NT for _ in range(NT)]
    for n in range(NT):
        for m in range(NT):
            if n != m:
                out[n][m] = 0.5 * (-1.0) ** (n - m) / math.sin(math.pi * (n - m) / NT)
    return out


@jax.custom_jvp
def recip(x):
    return 1.0 / x


@recip.defjvp
def recip_jvp(primals, tangents):
    r = recip(primals[0])
    return r, -(r * r) * tangents[0]


@jax.custom_jvp
def root(x):
    return x * lax.rsqrt(x)


@root.defjvp
def root_jvp(primals, tangents):
    x = primals[0]
    y = lax.rsqrt(x)
    return x * y, (0.5 * y) * tangents[0]


def prim(u):
    inv = recip(u[0])
    vel = [u[1] * inv, u[2] * inv, u[3] * inv]
    kin = u[1] * vel[0] + u[2] * vel[1] + u[3] * vel[2]
    return inv, vel, 0.4 * (u[4] - 0.5 * kin)


def faces(d, cells, shift):
    n = len(cells)
    base = [prim(u) for u in cells]
    p = [b[2] for b in base]
    q = {}
    for i in range(1, n - 1):
        u = cells[i]
        inv, vel, pres = base[i]
        temp = pres * inv
        rn = u[0] * u[5]
        ratio = rn * (1.0 / LAMINAR_MU)
        cube = ratio * ratio * ratio
        visc = LAMINAR_MU + rn * (cube * recip(cube + CV_CUBE))
        un = vel[d]
        flux = [un * u[v] for v in range(NV)]
        flux[1 + d] = flux[1 + d] + pres
        flux[4] = flux[4] + pres * un
        radius = root(un * un + 0.01) + root(1.4 * temp)
        square = vel[0] * vel[0] + vel[1] * vel[1] + vel[2] * vel[2]
        ends = p[i + 1] + p[i - 1]
        ratio_p = (ends - 2.0 * pres) * recip(ends + 2.0 * pres)
        q[i] = (vel, temp, rn, visc, flux, radius, 0.5 * square + HEAT_DIFFUSIVE * temp, ratio_p * ratio_p)
    out = []
    for a in range(1, n - 2):
        b = a + 1
        qa, qb = q[a], q[b]
        eps_two = SECOND_COEFF * 0.5 * (qa[7] + qb[7])
        eps_four = FOURTH_COEFF * FOURTH_COEFF * recip(FOURTH_COEFF + eps_two)
        spread = 0.5 * (qa[5] + qb[5])
        two, four = spread * eps_two, spread * eps_four
        isp = recip(1.0 + shift[b] - shift[a])
        mu = 0.5 * (qa[3] + qb[3]) * isp
        turb = (LAMINAR_MU + 0.5 * (qa[2] + qb[2])) * (1.0 / SIGMA_TURB) * isp
        face = []
        for v in range(NV):
            jump = cells[b][v] - cells[a][v]
            third = cells[b + 1][v] - cells[a - 1][v] - 3.0 * jump
            f = 0.5 * (qa[4][v] + qb[4][v]) - two * jump + four * third
            if 1 <= v <= 3:
                f = f - mu * (qb[0][v - 1] - qa[0][v - 1])
            elif v == 4:
                f = f - mu * (qb[6] - qa[6])
            elif v == 5:
                f = f - turb * jump
            face.append(f)
        out.append(face)
    return out, q[1][4]


def source(pitch_up, pitch_dn, span_up, span_dn, rad_up, rad_dn, rho, nu, inv_wall):
    def gap(up, dn, k):
        return 0.5 * (up[k] * recip(up[0]) - dn[k] * recip(dn[0]))

    cx = gap(span_up, span_dn, 2) - gap(rad_up, rad_dn, 2)
    cy = gap(rad_up, rad_dn, 1) - gap(pitch_up, pitch_dn, 2)
    cz = gap(pitch_up, pitch_dn, 1) - gap(span_up, span_dn, 1)
    vort = root(cx * cx + cy * cy + cz * cz + 0.01)
    scaled = nu * inv_wall
    return rho * (CW_ONE * scaled * scaled - PRODUCTION_COEF * vort * nu)


def kernel(sizes, state, adjoint, disp, out_state, out_disp,
           own, lam, dis, other, other_lam, other_dis,
           pit_lo, pit_hi, spa_lo, spa_hi, dpit_lo, dpit_hi, dspa_lo, dspa_hi,
           send_lo, send_hi, psend_lo, psend_hi, lsend, lrecv,
           upad, acc, gho, gacc, wbuf, dP, dS, dR, dG, cP, cS, cR, cG,
           rp_send_lo, rp_send_hi, rp_lo, rp_hi, rs_send_lo, rs_send_hi, rs_lo, rs_hi,
           rr_recv, rr_dsend, rr_drecv,
           local_sem, send_sem, recv_sem):
    n_pitch, n_span, n_rad, lanes = sizes
    ip = lax.axis_index("pitch")
    isp = lax.axis_index("span")
    ir = lax.axis_index("radial")
    ig = lax.axis_index("group")
    left = (ig, lax.rem(ip + n_pitch - 1, n_pitch), isp, ir)
    right = (ig, lax.rem(ip + 1, n_pitch), isp, ir)
    lower = (ig, ip, lax.rem(isp + n_span - 1, n_span), ir)
    upper = (ig, ip, lax.rem(isp + 1, n_span), ir)
    mate = (ig, ip, isp, 1 - ir)
    first = isp == 0
    last = isp == n_span - 1
    core0 = ir == 0

    loads = [
        pltpu.make_async_copy(state, own.at[pl.ds(0, NT * ROWS)], local_sem.at[0]),
        pltpu.make_async_copy(adjoint, lam.at[pl.ds(0, NT * ROWS)], local_sem.at[1]),
        pltpu.make_async_copy(disp, dis, local_sem.at[2]),
    ]
    for c in loads:
        c.start()

    bar = pltpu.get_barrier_semaphore()
    for who in (left, right, mate):
        pl.semaphore_signal(bar, inc=1, device_id=who, device_id_type=MESH)

    @pl.when(jnp.logical_not(first))
    def _():
        pl.semaphore_signal(bar, inc=1, device_id=lower, device_id_type=MESH)

    @pl.when(jnp.logical_not(last))
    def _():
        pl.semaphore_signal(bar, inc=1, device_id=upper, device_id_type=MESH)

    zero8 = jnp.zeros((8, lanes), jnp.float32)
    for v in range(NV):
        const = jnp.full((8, lanes), PAD_STATE[v], jnp.float32)
        for buf in (own, other):
            buf[pl.ds(NT * ROWS + v * CELLS, 8), :] = const
            buf[pl.ds(NT * ROWS + v * CELLS + 8, 8), :] = const
        for buf in (spa_lo, spa_hi):
            buf[pl.ds(NT * GROWS + v * 8, 8), :] = const
        for buf in (lam, other_lam):
            buf[pl.ds(NT * ROWS + v * CELLS, 8), :] = zero8
            buf[pl.ds(NT * ROWS + v * CELLS + 8, 8), :] = zero8

    sub = lax.broadcasted_iota(jnp.int32, (8, lanes), 0)
    for v in range(0, NV, 2):
        const = jnp.where(sub < 4, PAD_STATE[v], PAD_STATE[v + 1])
        for h in range(2):
            pit_hi[pl.ds(h * 8 * HROWS + NT * HROWS + v * 4, 8), :] = const
    const = jnp.where(sub < 4, jnp.where(sub < 2, PAD_STATE[2], PAD_STATE[3]),
                      jnp.where(sub < 6, PAD_STATE[4], PAD_STATE[5]))
    for h in range(2):
        pit_lo[pl.ds(h * 8 * QROWS + NT * QROWS + 4, 8), :] = const
        lrecv[pl.ds(h * 8 * QROWS + NT * QROWS + 4, 8), :] = zero8
    loads[0].wait()

    for p in range(4):
        for s in range(4):
            h, s2 = s // 2, s % 2
            for v in range(NV):
                x = own[pl.ds(v * CELLS + p * 4 + s, 8, stride=ROWS), :]
                upad[v, p + 2, s + 2] = x
                buf = send_lo if s < 2 else send_hi
                buf[pl.ds(v * 8 + p * 2 + s2, 8, stride=GROWS), :] = x
                if p < 2:
                    psend_lo[pl.ds(h * 8 * HROWS + v * 4 + p * 2 + s2, 8, stride=HROWS), :] = x
                if p == 3:
                    psend_hi[pl.ds(h * 8 * QROWS + v * 2 + s2, 8, stride=QROWS), :] = x

    loads[1].wait()
    for s in range(4):
        for v in range(NV):
            lsend[pl.ds((s // 2) * 8 * QROWS + v * 2 + s % 2, 8, stride=QROWS), :] = (
                lam[pl.ds(v * CELLS + s, 8, stride=ROWS), :])

    count = jnp.int32(3) + jnp.where(first, 0, 1) + jnp.where(last, 0, 1)
    pl.semaphore_wait(bar, count)

    def remote(k, src, dst, who):
        return pltpu.make_async_remote_copy(
            src_ref=src, dst_ref=dst, send_sem=send_sem.at[k], recv_sem=recv_sem.at[k],
            device_id=who, device_id_type=MESH)

    live = pl.ds(0, NT * GROWS)
    c_rstate = remote(0, own.at[pl.ds(0, NT * ROWS)], other.at[pl.ds(0, NT * ROWS)], mate)
    c_rlam = remote(1, lam.at[pl.ds(0, NT * ROWS)], other_lam.at[pl.ds(0, NT * ROWS)], mate)
    c_rdis = remote(2, dis.at[pl.ds(32, 16)], other_dis, mate)
    part = [pl.ds(h * 8 * HROWS, NT * HROWS) for h in range(2)]
    one_layer = [pl.ds(h * 8 * QROWS, NT * QROWS + 4) for h in range(2)]
    c_pup = [remote((3, 17)[h], psend_hi.at[one_layer[h]], pit_lo.at[one_layer[h]], right) for h in range(2)]
    c_lam = [remote((21, 22)[h], lsend.at[one_layer[h]], lrecv.at[one_layer[h]], left) for h in range(2)]
    c_pdn = [remote((4, 18)[h], psend_lo.at[part[h]], pit_hi.at[part[h]], left) for h in range(2)]
    c_dpup = remote(5, dis.at[pl.ds(8, 8)], dpit_lo, right)
    c_dpdn = remote(6, dis.at[pl.ds(0, 8)], dpit_hi, left)
    c_sup = remote(7, send_hi.at[live], spa_lo.at[live], upper)
    c_sdn = remote(8, send_lo.at[live], spa_hi.at[live], lower)
    c_dsup = remote(9, dis.at[pl.ds(16, 16)], dspa_lo, upper)
    c_dsdn = remote(10, dis.at[pl.ds(16, 16)], dspa_hi, lower)

    loads[2].wait()
    c_dpup.start()
    c_dpdn.start()
    c_pup[0].start()
    c_pdn[0].start()
    c_lam[0].start()
    c_rstate.start()
    c_rdis.start()

    @pl.when(jnp.logical_not(first))
    def _():
        c_sdn.start()
        c_dsdn.start()

    @pl.when(jnp.logical_not(last))
    def _():
        c_sup.start()
        c_dsup.start()

    c_pup[1].start()
    c_pdn[1].start()
    c_lam[1].start()
    c_rlam.start()

    coup = coupling_matrix()

    def w_loop(j, c):
        base = pl.multiple_of(j * 8, 8)
        rows = [lam[pl.ds(n * ROWS + base, 8), :] for n in range(NT)]
        for m in range(NT):
            t = None
            for n in range(NT):
                if n != m:
                    x = coup[n][m] * rows[n]
                    t = x if t is None else t + x
            wbuf[pl.ds(m * ROWS + base, 8), :] = t
        wbuf[pl.ds(NT * ROWS + base, 8), :] = zero8
        return c

    lax.fori_loop(0, ROWS // 8, w_loop, 0)

    def z_loop(i, c):
        for v in range(NV):
            for j in range(8):
                acc[v, i, j] = zero8
        return c

    lax.fori_loop(0, 8, z_loop, 0)
    for k in range(24):
        cP[k] = zero8
        cS[k] = zero8

    lane = lax.broadcasted_iota(jnp.int32, (8, lanes), 1)
    lane0 = lane == 0
    lane_last = lane == lanes - 1
    low2 = lane < 2
    high2 = lane >= lanes - 2
    one = jnp.where(core0, lanes - 1, 1)
    three = jnp.where(core0, lanes - 3, 3)
    cell = jnp.where(core0, lane, lanes - 1 - lane)
    from_mate = cell >= lanes - 2
    ghost_mate = cell < 2
    ends = jnp.logical_or(lane0, lane_last)

    def ghost(x, y):
        return jnp.where(ghost_mate, y, jnp.where(ends, pltpu.roll(x, one, 1), pltpu.roll(x, three, 1)))

    def unghost(g):
        return jnp.where(cell == 0, pltpu.roll(g, lanes - one, 1),
                         jnp.where(cell == 1, pltpu.roll(g, lanes - three, 1), 0.0))

    def up1(x, g):
        return pltpu.roll(jnp.where(lane0, g, x), lanes - 1, 1)

    def up2(x, g):
        return pltpu.roll(jnp.where(low2, g, x), lanes - 2, 1)

    def dn1(x, g):
        return pltpu.roll(jnp.where(lane_last, g, x), 1, 1)

    def back(cm, c0, c1, c2):
        x, g = c0, None
        for c, amount, mask in ((cm, lanes - 1, lane_last), (c1, 1, lane0), (c2, 2, low2)):
            if c is None:
                continue
            z = pltpu.roll(c, amount, 1)
            part = jnp.where(mask, 0.0, z)
            gpart = jnp.where(mask, z, 0.0)
            x = part if x is None else x + part
            g = gpart if g is None else g + gpart
        return x, g

    def wide(ref, i):
        return jnp.broadcast_to(ref[pl.ds(i, 1), :], (8, lanes))

    def lam_at(i, v):
        return lam[pl.ds(v * CELLS + i, 8, stride=ROWS), :]

    c_rstate.wait_recv()
    c_rdis.wait_recv()
    c_rlam.wait_recv()

    def rad_loop(i, carry):
        p, s = i // 4, i % 4
        x = [upad[v, p + 2, s + 2] for v in range(NV)]
        g = [ghost(x[v], other[pl.ds(v * CELLS + i, 8, stride=ROWS), :]) for v in range(NV)]
        for v in range(NV):
            gho[v, i] = g[v]
        sh = wide(dis, 32 + i)
        shg = ghost(sh, wide(other_dis, i))
        dG[i] = shg
        cot, wallcot = [], []
        for v in range(NV):
            a = lam_at(i, v)
            y = other_lam[pl.ds(v * CELLS + i, 8, stride=ROWS), :]
            y = jnp.where(core0, y, 0.0)
            cot.append(a - up1(a, y))
            wallcot.append(jnp.where(jnp.logical_and(core0, lane0), -a, 0.0))
        cells = [[dn1(x[v], g[v]) for v in range(NV)], x,
                 [up1(x[v], g[v]) for v in range(NV)], [up2(x[v], g[v]) for v in range(NV)]]

        def f(cells, s1, s2):
            o, w = faces(2, cells, {1: s1, 2: s2})
            return o[0], w

        _, pull = jax.vjp(f, cells, sh, up1(sh, shg))
        bar_cells, b1, b2 = pull((cot, wallcot))
        for v in range(NV):
            xb, gb = back(bar_cells[0][v], bar_cells[1][v], bar_cells[2][v], bar_cells[3][v])
            acc[v, p + 2, s + 2] = xb
            gacc[v, i] = gb
        xb, gb = back(None, b1, b2, None)
        cR[i] = xb
        cG[i] = gb
        return carry

    lax.fori_loop(0, CELLS, rad_loop, 0)

    @pl.when(first)
    def _():
        def body(p, c):
            for v in range(NV):
                upad[v, p + 2, 1] = upad[v, p + 2, 2]
                upad[v, p + 2, 0] = upad[v, p + 2, 3]
            dS[pl.ds(p, 1), :] = dis[pl.ds(16 + p * 4, 1), :]
            return c
        lax.fori_loop(0, 4, body, 0)

    @pl.when(jnp.logical_not(first))
    def _():
        c_sup.wait_recv()
        c_dsup.wait_recv()

        def body(p, c):
            for v in range(NV):
                for s in range(2):
                    upad[v, p + 2, s] = spa_lo[pl.ds(v * 8 + p * 2 + s, 8, stride=GROWS), :]
            dS[pl.ds(p, 1), :] = dspa_lo[pl.ds(p * 4 + 3, 1), :]
            return c
        lax.fori_loop(0, 4, body, 0)

    @pl.when(last)
    def _():
        def body(p, c):
            for v in range(NV):
                upad[v, p + 2, 6] = upad[v, p + 2, 5]
                upad[v, p + 2, 7] = upad[v, p + 2, 4]
            dS[pl.ds(20 + p, 1), :] = dis[pl.ds(16 + p * 4 + 3, 1), :]
            return c
        lax.fori_loop(0, 4, body, 0)

    @pl.when(jnp.logical_not(last))
    def _():
        c_sdn.wait_recv()
        c_dsdn.wait_recv()

        def body(p, c):
            for v in range(NV):
                for s in range(2):
                    upad[v, p + 2, 6 + s] = spa_hi[pl.ds(v * 8 + p * 2 + s, 8, stride=GROWS), :]
            dS[pl.ds(20 + p, 1), :] = dspa_hi[pl.ds(p * 4, 1), :]
            return c
        lax.fori_loop(0, 4, body, 0)

    for k in range(4):
        for p in range(4):
            dS[pl.ds((k + 1) * 4 + p, 1), :] = dis[pl.ds(16 + p * 4 + k, 1), :]
            dP[pl.ds((k + 1) * 4 + p, 1), :] = dis[pl.ds(k * 4 + p, 1), :]

    def line(d, cells, shift, lams):
        cot = []
        for i in range(1, 6):
            row = []
            for v in range(NV):
                if i == 1:
                    row.append(-lams[0][v])
                elif i == 5:
                    row.append(lams[3][v])
                else:
                    row.append(lams[i - 2][v] - lams[i - 1][v])
            cot.append(row)
        _, pull = jax.vjp(lambda c, s: faces(d, c, dict(zip(range(1, 7), s)))[0], cells, shift)
        return pull(cot)

    pos = (ir * lanes + lane).astype(jnp.float32) + 0.5
    inv_wall = 1.0 / jnp.minimum(pos, n_rad * lanes - pos)

    def cell_work(p, s):
        i = p * 4 + s
        a, b = p + 2, s + 2
        x = [upad[v, a, b] for v in range(NV)]
        g = [gho[v, i] for v in range(3)]
        pu = [upad[v, a + 1, b] for v in (0, 2, 3)]
        pd = [upad[v, a - 1, b] for v in (0, 2, 3)]
        su = [upad[v, a, b + 1] for v in (0, 1, 3)]
        sd = [upad[v, a, b - 1] for v in (0, 1, 3)]
        ru = [up1(x[v], g[v]) for v in (0, 1, 2)]
        rd = [dn1(x[v], g[v]) for v in (0, 1, 2)]
        _, pull = jax.vjp(lambda *t: source(*t, inv_wall), pu, pd, su, sd, ru, rd, x[0], x[5])
        bpu, bpd, bsu, bsd, bru, brd, brho, bnu = pull(lam_at(i, 5))
        ghosts_to, terms = [], []
        extra = [brho, None, None, None, None, bnu]
        for j, v in enumerate((0, 1, 2)):
            xb, gb = back(brd[j], extra[v], bru[j], None)
            extra[v] = xb
            ghosts_to.append(gb)
        dpu, dpd = wide(dP, (p + 2) * 4 + s), wide(dP, p * 4 + s)
        dsu, dsd = wide(dS, (s + 2) * 4 + p), wide(dS, s * 4 + p)
        sh, shg = wide(dis, 32 + i), dG[i]
        f0 = 1.0 + 0.5 * (dpu - dpd)
        f1 = 1.0 + 0.5 * (dsu - dsd)
        f2 = 1.0 + 0.5 * (up1(sh, shg) - dn1(sh, shg))
        f01 = f0 * f1
        vol = FREQUENCY * f01 * f2
        vbar = None
        for v in range(NV):
            w = wbuf[pl.ds(v * CELLS + i, 8, stride=ROWS), :]
            t = vol * w
            if extra[v] is not None:
                t = t + extra[v]
            terms.append(t)
            vbar = w * x[v] if vbar is None else vbar + w * x[v]
        h = (0.5 * FREQUENCY) * vbar
        h0 = h * (f1 * f2)
        h1 = h * (f0 * f2)
        h2 = h * f01
        xb, gb = back(-h2, None, h2, None)

        def add():
            for j, v in enumerate((0, 2, 3)):
                acc[v, a + 1, b] += bpu[j]
                acc[v, a - 1, b] += bpd[j]
            for j, v in enumerate((0, 1, 3)):
                acc[v, a, b + 1] += bsu[j]
                acc[v, a, b - 1] += bsd[j]
            for v in range(3):
                gacc[v, i] += ghosts_to[v]
            for v in range(NV):
                acc[v, a, b] += terms[v]
            cP[(p + 2) * 4 + s] += h0
            cP[p * 4 + s] -= h0
            cS[(s + 2) * 4 + p] += h1
            cS[s * 4 + p] -= h1
            cR[i] += xb
            cG[i] += gb

        return add

    def pitch_line(s, h, s2):
        cells = [[upad[v, k, s + 2] for v in range(NV)] for k in range(1, 8)]
        shift = [wide(dP, k * 4 + s) for k in range(1, 6)]
        lams = [[lam_at(k * 4 + s, v) for v in range(NV)] for k in range(4)]
        lams.append([lrecv[pl.ds(h * 8 * QROWS + v * 2 + s2, 8, stride=QROWS), :] for v in range(NV)])
        cot = [[lams[k][v] - lams[k + 1][v] for v in range(NV)] for k in range(4)]
        _, pull = jax.vjp(lambda c, t: faces(0, c, dict(zip(range(1, 6), t)))[0], cells, shift)
        bc, bs = pull(cot)
        for k in range(7):
            for v in range(NV):
                acc[v, k + 1, s + 2] += bc[k][v]
        for k in range(5):
            cP[(k + 1) * 4 + s] += bs[k]

    def total(x):
        return jnp.sum(x, axis=0, keepdims=True)

    back_part = [pl.ds(h * 8 * HROWS, NT * HROWS + 8) for h in range(2)]
    r_pup = [remote((11, 19)[h], rp_send_hi.at[back_part[h]], rp_lo.at[back_part[h]], right) for h in range(2)]
    r_pdn = [remote((12, 20)[h], rp_send_lo.at[one_layer[h]], rp_hi.at[one_layer[h]], left) for h in range(2)]

    def chunk(h):
        c_pup[h].wait_recv()
        c_pdn[h].wait_recv()
        c_lam[h].wait_recv()
        if h == 0:
            c_dpup.wait_recv()
            c_dpdn.wait_recv()
            for s in range(4):
                dP[pl.ds(s, 1), :] = dpit_lo[pl.ds(4 + s, 1), :]
                dP[pl.ds(20 + s, 1), :] = dpit_hi[pl.ds(s, 1), :]

        def ghosts(s2, c):
            s = 2 * h + s2
            for v in range(NV):
                upad[v, 1, s + 2] = pit_lo[pl.ds(h * 8 * QROWS + v * 2 + s2, 8, stride=QROWS), :]
                for k in range(2):
                    row = pl.ds(h * 8 * HROWS + v * 4 + k * 2 + s2, 8, stride=HROWS)
                    upad[v, 6 + k, s + 2] = pit_hi[row, :]
            pitch_line(s, h, s2)
            return c

        lax.fori_loop(0, 2, ghosts, 0)

        def cells_loop(p, c):
            adds = [cell_work(p, 2 * h), cell_work(p, 2 * h + 1)]
            for add in adds:
                add()
            return c

        lax.fori_loop(0, 4, cells_loop, 0)

        base = h * 8 * HROWS
        low = h * 8 * QROWS
        for s2 in range(2):
            s = 2 * h + s2
            for v in range(NV):
                rp_send_lo[pl.ds(low + v * 2 + s2, 8, stride=QROWS), :] = acc[v, 1, s + 2]
                for k in range(2):
                    rp_send_hi[pl.ds(base + v * 4 + k * 2 + s2, 8, stride=HROWS), :] = acc[v, 6 + k, s + 2]
        for s2 in range(2):
            rp_send_lo[pl.ds(low + NT * QROWS + s2, 1), :] = total(cP[2 * h + s2])
            rp_send_hi[pl.ds(base + NT * HROWS + s2, 1), :] = total(cP[20 + 2 * h + s2])
        r_pup[h].start()
        r_pdn[h].start()

    chunk(0)

    def span_loop(p, carry):
        cells = [[upad[v, p + 2, k] for v in range(NV)] for k in range(8)]
        shift = [wide(dS, k * 4 + p) for k in range(6)]
        lams = [[lam_at(p * 4 + k, v) for v in range(NV)] for k in range(4)]
        bc, bs = line(1, cells, shift, lams)
        for k in range(8):
            for v in range(NV):
                acc[v, p + 2, k] += bc[k][v]
        for k in range(6):
            cS[k * 4 + p] += bs[k]
        return carry

    lax.fori_loop(0, 4, span_loop, 0)

    chunk(1)

    gone = NT * GROWS + 8
    sent = pl.ds(0, gone)

    def spa_pack(p, c):
        for v in range(NV):
            for k in range(2):
                rs_send_lo[pl.ds(v * 8 + p * 2 + k, 8, stride=GROWS), :] = acc[v, p + 2, k]
                rs_send_hi[pl.ds(v * 8 + p * 2 + k, 8, stride=GROWS), :] = acc[v, p + 2, 6 + k]
        return c

    lax.fori_loop(0, 4, spa_pack, 0)
    for buf in (rs_send_lo, rs_send_hi):
        buf[pl.ds(NT * GROWS, 8), :] = zero8
    for p in range(4):
        rs_send_lo[pl.ds(NT * GROWS + p, 1), :] = total(cS[p])
        rs_send_hi[pl.ds(NT * GROWS + p, 1), :] = total(cS[20 + p])
    r_sup = remote(13, rs_send_hi.at[sent], rs_lo.at[sent], upper)
    r_sdn = remote(14, rs_send_lo.at[sent], rs_hi.at[sent], lower)

    @pl.when(jnp.logical_not(first))
    def _():
        r_sdn.start()

    @pl.when(jnp.logical_not(last))
    def _():
        r_sup.start()

    for i in range(CELLS):
        rr_dsend[pl.ds(i, 1), :] = total(cG[i])
    r_rad = remote(15, gacc, rr_recv, mate)
    r_rdis = remote(16, rr_dsend, rr_drecv, mate)
    r_rad.start()
    r_rdis.start()

    for p in range(4):
        for s in range(4):
            out_disp[pl.ds(p * 4 + s, 1), :] = total(cP[(p + 1) * 4 + s])
            out_disp[pl.ds(16 + p * 4 + s, 1), :] = total(cS[(s + 1) * 4 + p])
            out_disp[pl.ds(32 + p * 4 + s, 1), :] = total(cR[p * 4 + s] + unghost(cG[p * 4 + s]))

    @pl.when(first)
    def _():
        def body(p, c):
            for v in range(NV):
                acc[v, p + 2, 2] += acc[v, p + 2, 1]
                acc[v, p + 2, 3] += acc[v, p + 2, 0]
            out_disp[pl.ds(16 + p * 4, 1), :] += rs_send_lo[pl.ds(NT * GROWS + p, 1), :]
            return c
        lax.fori_loop(0, 4, body, 0)

    @pl.when(last)
    def _():
        def body(p, c):
            for v in range(NV):
                acc[v, p + 2, 5] += acc[v, p + 2, 6]
                acc[v, p + 2, 4] += acc[v, p + 2, 7]
            out_disp[pl.ds(16 + p * 4 + 3, 1), :] += rs_send_hi[pl.ds(NT * GROWS + p, 1), :]
            return c
        lax.fori_loop(0, 4, body, 0)

    r_rad.wait_recv()
    r_rdis.wait_recv()

    def rad_finish(i, c):
        p, s = i // 4, i % 4
        for v in range(NV):
            acc[v, p + 2, s + 2] += unghost(gacc[v, i]) + jnp.where(from_mate, rr_recv[v, i], 0.0)
        return c

    lax.fori_loop(0, CELLS, rad_finish, 0)
    for j in range(2):
        out_disp[pl.ds(32 + 8 * j, 8), :] += jnp.where(from_mate, rr_drecv[pl.ds(8 * j, 8), :], 0.0)

    @pl.when(jnp.logical_not(first))
    def _():
        r_sup.wait_recv()

        def body(p, c):
            for v in range(NV):
                for k in range(2):
                    acc[v, p + 2, 2 + k] += rs_lo[pl.ds(v * 8 + p * 2 + k, 8, stride=GROWS), :]
            out_disp[pl.ds(16 + p * 4, 1), :] += rs_lo[pl.ds(NT * GROWS + p, 1), :]
            return c
        lax.fori_loop(0, 4, body, 0)

    @pl.when(jnp.logical_not(last))
    def _():
        r_sdn.wait_recv()

        def body(p, c):
            for v in range(NV):
                for k in range(2):
                    acc[v, p + 2, 4 + k] += rs_hi[pl.ds(v * 8 + p * 2 + k, 8, stride=GROWS), :]
            out_disp[pl.ds(16 + p * 4 + 3, 1), :] += rs_hi[pl.ds(NT * GROWS + p, 1), :]
            return c
        lax.fori_loop(0, 4, body, 0)

    for h in range(2):
        r_pup[h].wait_recv()
        r_pdn[h].wait_recv()
        for s2 in range(2):
            s = 2 * h + s2
            for v in range(NV):
                for p in range(4):
                    x = acc[v, p + 2, s + 2]
                    if p < 2:
                        x = x + rp_lo[pl.ds(h * 8 * HROWS + v * 4 + p * 2 + s2, 8, stride=HROWS), :]
                    if p == 3:
                        x = x + rp_hi[pl.ds(h * 8 * QROWS + v * 2 + s2, 8, stride=QROWS), :]
                    out_state[pl.ds(v * CELLS + p * 4 + s, NT, stride=ROWS), :] = x[:NT]
            out_disp[pl.ds(s, 1), :] += rp_lo[pl.ds(h * 8 * HROWS + NT * HROWS + s2, 1), :]
            out_disp[pl.ds(12 + s, 1), :] += rp_hi[pl.ds(h * 8 * QROWS + NT * QROWS + s2, 1), :]

    for c in (c_rstate, c_rlam, c_rdis, *c_pup, *c_pdn, *c_lam, c_dpup, c_dpdn, *r_pup, *r_pdn, r_rad, r_rdis):
        c.wait_send()

    @pl.when(jnp.logical_not(first))
    def _():
        for c in (c_sdn, c_dsdn, r_sdn):
            c.wait_send()

    @pl.when(jnp.logical_not(last))
    def _():
        for c in (c_sup, c_dsup, r_sup):
            c.wait_send()


def solution(mesh):
    def body(state, adjoint, displacement):
        lanes = state.shape[-1]
        sizes = (mesh.shape["pitch"], mesh.shape["span"], mesh.shape["radial"], lanes)
        f32 = jnp.float32

        def vm(*lead):
            return pltpu.VMEM(tuple(lead) + (lanes,), f32)

        scratch = [
            vm(8 * ROWS), vm(8 * ROWS), vm(48), vm(8 * ROWS), vm(8 * ROWS), vm(16),
            vm(8 * GROWS), vm(8 * GROWS), vm(8 * GROWS), vm(8 * GROWS), vm(8), vm(8), vm(16), vm(16),
            vm(8 * GROWS), vm(8 * GROWS), vm(8 * GROWS), vm(8 * GROWS), vm(8 * GROWS), vm(8 * GROWS),
            vm(NV, 8, 8, 8), vm(NV, 8, 8, 8), vm(NV, CELLS, 8), vm(NV, CELLS, 8), vm(8 * ROWS),
            vm(24), vm(24), vm(16), vm(16, 8), vm(24, 8), vm(24, 8), vm(16, 8), vm(16, 8),
            vm(8 * GROWS), vm(8 * GROWS), vm(8 * GROWS), vm(8 * GROWS),
            vm(8 * GROWS), vm(8 * GROWS), vm(8 * GROWS), vm(8 * GROWS),
            vm(NV, CELLS, 8), vm(16), vm(16),
            pltpu.SemaphoreType.DMA((3,)), pltpu.SemaphoreType.DMA((23,)), pltpu.SemaphoreType.DMA((23,)),
        ]
        any_spec = pl.BlockSpec(memory_space=pl.ANY)
        vmem_spec = pl.BlockSpec(memory_space=pltpu.VMEM)
        out_state, out_disp = pl.pallas_call(
            lambda *refs: kernel(sizes, *refs),
            out_shape=(
                jax.ShapeDtypeStruct((NT * ROWS, lanes), f32),
                jax.ShapeDtypeStruct((3 * CELLS, lanes), f32),
            ),
            in_specs=[any_spec] * 3,
            out_specs=(vmem_spec, vmem_spec),
            scratch_shapes=scratch,
            compiler_params=pltpu.CompilerParams(
                collective_id=0, has_side_effects=True, vmem_limit_bytes=60 * 1024 * 1024),
            name="adjoint",
        )(
            state.reshape(NT * ROWS, lanes),
            adjoint.reshape(NT * ROWS, lanes),
            displacement.reshape(3 * CELLS, lanes),
        )
        return out_state.reshape(state.shape), out_disp.reshape(displacement.shape)

    spec = P("group", None, "pitch", "span", "radial")
    dspec = P("group", "pitch", "span", "radial")
    return jax.shard_map(
        body, mesh=mesh, in_specs=(spec, spec, dspec), out_specs=(spec, dspec), check_vma=False)
```
